256 devices in a mesh: ctx: 64 (over z, x, y_lo), head: 4 (over y_hi, core).
Axes of the slice: x: 4, y: 4 (y_hi: 2, y_lo: 2; y = y_hi * 2 + y_lo), z: 8, core: 2. Of those that a mesh axis runs over, the one named last changes fastest.
Arguments:
- query: float32 [8192, 1536], P('ctx', 'head'), may hold values from -240 to 240
- key: float32 [8192, 1536], P('ctx', 'head'), may hold values from -6 to 6
- value: float32 [8192, 1536], P('ctx', 'head'), may hold values from -6 to 6
- segment: int32 [8192], P('ctx'), may hold values from 0 to 31, never falling along the last dimension, each value on 1 to 768 neighbouring positions
- band: int32 [16], replicated, may hold values from 1 to 3, as said below
- out_weight: float32 [1536, 1536], P('head'), may hold values from -0.15625 to 0.15625
- cotangent: float32 [8192, 1536], P('ctx', 'head'), may hold values from -16 to 16
Outputs:
- output: float32 [8192, 1536], P('ctx', 'head')
- grad_query: float32 [8192, 1536], P('ctx', 'head')
- grad_key: float32 [8192, 1536], P('ctx', 'head')
- grad_value: float32 [8192, 1536], P('ctx', 'head')
- grad_weight: float32 [1536, 1536], P('head', 'ctx')
The draws below stay inside these ranges and needn't reach their ends.
Inputs may be any that keep to these rules, and one draw needn't show every extreme that they name: A head attends to keys at most band blocks from the query's block; some head has band 3. `segment`: utterance numbers never fall along the frames.
All inputs are finite; a program needn't handle non-finite values.
Results may differ from the reference program's by a relative error of at most 0.0003.
Values sent between devices are 32-bit elements; how exact they have to be, the bound alone decides.
A program may use at most 64 MiB of HBM per device.

```python
import math
import jax
import jax.numpy as jnp
import numpy as np
from jax import lax

D = 1536
HEADS = 16
HEAD_DIM = 96
BLOCK = 128
REACH = 3
FRAMES = 8192


def shared_normal(key):
    return jax.random.normal(key, (FRAMES, D), jnp.float32)


def draw_key(key, part):
    base = jnp.clip(shared_normal(key), -6.0, 6.0)
    return base


def draw_query(key, part):
    key = jax.random.fold_in(key, 7)
    return jnp.clip(jax.random.normal(key, (FRAMES, D), jnp.float32), -6.0, 6.0)


def draw_band(key, part):
    key = jax.random.fold_in(key, 5)
    widths = jax.random.randint(key, (HEADS,), 1, REACH + 1, jnp.int32)
    chosen = jax.random.randint(jax.random.fold_in(key, 1), (), 0, HEADS, jnp.int32)
    return widths.at[chosen].set(REACH)


def spiked(values, key, source, target, parts, factor):
    owner, partner = [(jnp.arange(values.shape[axis_at]) // (values.shape[axis_at] // parts)).reshape([-1 if axis == axis_at else 1 for axis in range(values.ndim)]) for axis_at in (source, target)]
    chosen = jax.random.permutation(key, parts)[partner]
    strong = (owner == chosen) | (owner == (partner + parts // 2) % parts)
    return jnp.where(strong, factor * values, values)


def steps_of(rng, dims, cuts, least, top_value):
    level, own = 1.0, jax.random.fold_in(rng, 6)
    for dim, shards_of in cuts:
        draws = jnp.exp(jax.random.uniform(jax.random.fold_in(own, dim), (shards_of,), jnp.float32, least / len(cuts), top_value / len(cuts)))
        level = level * jnp.repeat(draws, dims[dim] // shards_of).reshape([-1 if axis == dim else 1 for axis in range(len(dims))])
    return level


def profile(number_of, total, most, skew):
    loads = [(1 << 20) // math.isqrt(grade ** skew) + 1 for grade in range(2, number_of + 1)]
    surplus, holding = total - most - (number_of - 1), [1] * (number_of - 1)
    while surplus > 0:
        movable = [i for i in range(number_of - 1) if holding[i] < most]
        whole, budget = sum([loads[i] for i in movable]), surplus
        for i in movable:
            more = min(most - holding[i], max(1, budget * loads[i] // whole), surplus)
            holding[i] = holding[i] + more
            surplus = surplus - more
    return np.array([most] + holding)


def uneven(rng, count, total, limit, slope):
    if count == 2:
        one = jax.random.randint(rng, (), max(1, total - limit), min(limit, total - 1) + 1)
        return jnp.stack([one, total - one])
    lengths = jnp.asarray(profile(count, total, limit, slope), jnp.int32)
    pairs = (count - 1) // 2
    donor, taker = lengths[1:1 + 2 * pairs:2], lengths[2:2 + 2 * pairs:2]
    slack = jnp.minimum(donor - 1, limit - taker)
    passed = jax.random.randint(jax.random.fold_in(rng, 1), (pairs,), 0, 1 << 20) % (slack + 1)
    lengths = lengths.at[1:1 + 2 * pairs:2].set(donor - passed).at[2:2 + 2 * pairs:2].set(taker + passed)
    return lengths[jax.random.permutation(jax.random.fold_in(rng, 2), count)]


def normal_values(own_key, shape, deviation, most, shards=(), held_as=jnp.bfloat16):
    array = jax.random.normal(own_key, shape, jnp.float32) * deviation
    if len(shards) > 0:
        array = steps_of(own_key, shape, shards, -0.22, 0.18) * array
    return jnp.clip(array, min=-most, max=most).astype(held_as)


def gaussian_with(own_key, extent, deviation, bound, cuts, heavy, kind=jnp.bfloat16):
    values = deviation * jax.random.normal(own_key, extent, jnp.float32)
    if cuts:
        values = values * steps_of(own_key, extent, cuts, -0.22, 0.18)
    return jnp.clip(spiked(values, jax.random.fold_in(own_key, 3), *heavy), -bound, bound).astype(kind)


def setup_inputs(seed: int = 0) -> dict:
    key_list = jax.random.split(jax.random.key(seed), 8)
    query = draw_query(jax.random.fold_in(key_list[7], 71), 0)
    key = draw_key(jax.random.fold_in(key_list[7], 71), 0)
    value = normal_values(key_list[2], (FRAMES, D), 1.0, 6.0, ((0, 64), (1, 4)), jnp.float32)
    segment = jnp.searchsorted(jnp.cumsum(uneven(key_list[3], FRAMES // (2 * BLOCK), FRAMES, 6 * BLOCK, 2)), jnp.arange(FRAMES), side="right").astype(jnp.int32)
    band = draw_band(jax.random.fold_in(key_list[7], 71), 0)
    out_weight = normal_values(key_list[5], (D, D), D ** -0.5, 0.15625, ((0, 4),), jnp.float32)
    cotangent = gaussian_with(key_list[6], (FRAMES, D), 1.0, 16.0, ((0, 64), (1, 4)), (0, 1, 64, 4.0), jnp.float32)
    return dict(query=query, key=key, value=value, segment=segment, band=band, out_weight=out_weight, cotangent=cotangent)


def reference(query, key, value, segment, band, out_weight, cotangent):
    scale = 1.0 / math.sqrt(HEAD_DIM)
    blocks = FRAMES // BLOCK
    window = (2 * REACH + 1) * BLOCK
    margin = REACH * BLOCK
    highest = lax.Precision.HIGHEST
    key_padded = jnp.pad(key, ((margin, margin), (0, 0)))
    value_padded = jnp.pad(value, ((margin, margin), (0, 0)))
    labels = (segment + 1).astype(jnp.int32)
    label_padded = jnp.pad(labels, (margin, margin))
    offsets = jnp.arange(window, dtype=jnp.int32) // BLOCK - REACH
    within = jnp.abs(offsets)[None, :] <= band[:, None]

    def pieces(index):
        start = (index * BLOCK).astype(jnp.int32)
        query_block = lax.dynamic_slice_in_dim(query, start, BLOCK, 0).reshape(BLOCK, HEADS, HEAD_DIM)
        keys_near = lax.dynamic_slice_in_dim(key_padded, start, window, 0).reshape(window, HEADS, HEAD_DIM)
        values_near = lax.dynamic_slice_in_dim(value_padded, start, window, 0).reshape(window, HEADS, HEAD_DIM)
        labels_near = lax.dynamic_slice_in_dim(label_padded, start, window, 0)
        labels_here = lax.dynamic_slice_in_dim(labels, start, BLOCK, 0)
        allowed = (labels_here[:, None] == labels_near[None, :])[None, :, :] & within[:, None, :]
        scores = jnp.einsum('ihe,jhe->hij', query_block, keys_near, precision=highest) * scale
        scores = jnp.where(allowed, scores, -1e+30)
        return (query_block, keys_near, values_near, allowed, scores)

    def forward_block(index):
        query_block, keys_near, values_near, allowed, scores = pieces(index)
        largest = lax.optimization_barrier(jnp.max(scores, axis=2))
        weights = jnp.where(allowed, jnp.exp(scores - largest[:, :, None]), 0.0)
        total = lax.optimization_barrier(jnp.sum(weights, axis=2))
        mixed = jnp.einsum('hij,jhe->ihe', weights, values_near, precision=highest) / total.T[:, :, None]
        return (mixed.reshape(BLOCK, D), largest + jnp.log(total))
    indices = jnp.arange(blocks, dtype=jnp.int32)
    attended, log_totals = lax.map(forward_block, indices)
    attended = attended.reshape(FRAMES, D)
    output = jnp.dot(attended, out_weight, precision=highest)
    grad_attended = jnp.dot(cotangent, out_weight.T, precision=highest)
    grad_weight = jnp.dot(attended.T, cotangent, precision=highest)

    def backward_block(carry, inputs):
        index, log_total = inputs
        grad_keys, grad_values = carry
        query_block, keys_near, values_near, allowed, scores = pieces(index)
        start = (index * BLOCK).astype(jnp.int32)
        grad_block = lax.dynamic_slice_in_dim(grad_attended, start, BLOCK, 0).reshape(BLOCK, HEADS, HEAD_DIM)
        mixed_block = lax.dynamic_slice_in_dim(attended, start, BLOCK, 0).reshape(BLOCK, HEADS, HEAD_DIM)
        probs = jnp.where(allowed, jnp.exp(scores - log_total[:, :, None]), 0.0)
        delta = lax.optimization_barrier(jnp.sum(grad_block * mixed_block, axis=2)).T
        value_part = jnp.einsum('hij,ihe->jhe', probs, grad_block, precision=highest)
        grad_probs = jnp.einsum('ihe,jhe->hij', grad_block, values_near, precision=highest)
        grad_scores = probs * (grad_probs - delta[:, :, None])
        query_part = scale * jnp.einsum('hij,jhe->ihe', grad_scores, keys_near, precision=highest)
        key_part = scale * jnp.einsum('hij,ihe->jhe', grad_scores, query_block, precision=highest)
        old_keys = lax.dynamic_slice_in_dim(grad_keys, start, window, 0)
        grad_keys = lax.dynamic_update_slice_in_dim(grad_keys, old_keys + key_part.reshape(window, D), start, 0)
        old_values = lax.dynamic_slice_in_dim(grad_values, start, window, 0)
        grad_values = lax.dynamic_update_slice_in_dim(grad_values, old_values + value_part.reshape(window, D), start, 0)
        return ((grad_keys, grad_values), query_part.reshape(BLOCK, D))
    empty = jnp.zeros((FRAMES + 2 * margin, D), jnp.float32)
    (grad_keys, grad_values), grad_query = lax.scan(backward_block, (empty, empty), (indices, log_totals))
    grad_key = grad_keys[margin:margin + FRAMES]
    grad_value = grad_values[margin:margin + FRAMES]
    return (output, grad_query.reshape(FRAMES, D), grad_key, grad_value, grad_weight)
```

```python
import math

import jax
import jax.numpy as jnp
from jax import lax
from jax.experimental import pallas as pl
from jax.experimental.pallas import tpu as pltpu
from jax.sharding import PartitionSpec as P

MESH = pl.DeviceIdType.MESH
F32 = jnp.float32
BF16 = jnp.bfloat16
HD = 96
SCALE = 1.0 / math.sqrt(HD)
B = 128
W8 = 8 * B
NZ, NX = 8, 4
CHUNK = 32


def split2(x):
    hi = x.astype(BF16)
    return hi, (x - hi.astype(F32)).astype(BF16)


def split3(x):
    hi = x.astype(BF16)
    rest = x - hi.astype(F32)
    mid = rest.astype(BF16)
    return hi, mid, (rest - mid.astype(F32)).astype(BF16)


def dot(a, b):
    return jnp.dot(a, b, preferred_element_type=F32)


def dot_nt(a, b):
    return lax.dot_general(a, b, (((1,), (1,)), ((), ())), preferred_element_type=F32)


def pad_rows(x):
    return jnp.concatenate([x, jnp.zeros((B - HD, x.shape[1]), x.dtype)], axis=0)


def mul6(left, right):
    lh, lm, ll = split3(left)
    rh, rm, rl = split3(right)
    return dot(
        jnp.concatenate([lh, lh, lm, lm, lh, ll], axis=1),
        jnp.concatenate([rh, rm, rh, rm, rl, rh], axis=0),
    )


def mul4(left, right):
    lh, lm = split2(left)
    rh, rm = split2(right)
    return dot(
        jnp.concatenate([lh, lh, lm, lm], axis=1),
        jnp.concatenate([rh, rm, rh, rm], axis=0),
    )


def mul_window(hi, mid, right):
    rh, rm = split2(right)
    both = jnp.concatenate([rh, rm], axis=0)
    out = dot_nt(hi, both) + dot_nt(mid, both)
    return out[:, :B] + out[:, B:]


def mul3(lh, lm, rh, rm):
    return dot(lh, rh) + (dot(lh, rm) + dot(lm, rh))


def kernel(
    q_ref, k_ref, v_ref, seg_ref, band_ref, w_ref, cot_ref,
    out_ref, gq_ref, gk_ref, gv_ref, gw_ref,
    tq, tkv, kvs, kvw, qs, qw, dow, stw, cotw, wv, lab_col, lab_row,
    coth, cotm, cotth, cottm, wh, wm,
    s_ref, e_ref, dp_ref, ph, pm, col_ref, att_t, do_t, ath, atm,
    po, por, ps, pr, mx, xr, xs, zr, gsum, yr, gown, gsend, grecv,
    ss, kv_sem, q_sem, do_sem, st_sem, cot_sem, y_sem, po_sem, pr_sem, x_sem, z_sem, g_sem, w_sem,
):
    ctx = lax.axis_index("ctx")
    head = lax.axis_index("head")
    yl = ctx % 2
    pair_index = ctx // 2
    z, x = pair_index // NX, pair_index % NX
    core = head % 2
    y = (head // 2) * 2 + yl
    other = 1 - yl

    def at(z_, x_, y_, c_):
        return ((z_ * NX + x_) * 2 + y_ % 2, (y_ // 2) * 2 + c_)

    def pair(k):
        p = (pair_index + k + NZ * NX) % (NZ * NX)
        return at(p // NX, p % NX, y, core)

    partner = at(z, x, (head // 2) * 2 + other, core)
    sibling = at(z, x, y, 1 - core)

    def along_y(k):
        return at(z, x, (y + k) % 4, core)

    def along_x(k):
        return at(z, (x + k) % NX, y, core)

    def along_z(k):
        return at((z + k) % NZ, x, y, core)

    peers = [pair(k) for k in (1, -1, 2, -2)]
    peers += [along_y(k) for k in (1, 2, 3)] + [sibling]
    peers += [along_x(k) for k in (1, 2, 3)]
    peers += [along_z(k) for k in range(1, NZ)]
    barrier = pltpu.get_barrier_semaphore()
    for peer in peers:
        pl.semaphore_signal(barrier, inc=1, device_id=peer, device_id_type=MESH)

    w_copy = pltpu.make_async_copy(
        w_ref.at[pl.ds(pl.multiple_of(yl * 192, 8), 192)], wv, w_sem
    )
    w_copy.start()

    pending = []

    def send(src, dst, recv_sem, device):
        copy = pltpu.make_async_remote_copy(
            src_ref=src, dst_ref=dst, send_sem=ss.at[len(pending)], recv_sem=recv_sem,
            device_id=device, device_id_type=MESH,
        )
        copy.start()
        pending.append(copy)

    def arrived(dst, recv_sem):
        pltpu.make_async_remote_copy(
            src_ref=dst, dst_ref=dst, send_sem=ss.at[0], recv_sem=recv_sem,
            device_id=partner, device_id_type=MESH,
        ).wait_recv()

    own = 3 + yl
    theirs = 3 + other

    mine = pl.ds(pl.multiple_of(yl * 192, 8), 192)
    rest = pl.ds(pl.multiple_of(other * 192, 8), 192)
    tkv[0] = k_ref[...].T
    tkv[1] = v_ref[...].T
    tq[...] = (q_ref[...] * SCALE).T
    label = jnp.broadcast_to((seg_ref[...] + 1).astype(F32), (8, B))
    kvs[0:192] = tkv[0, rest]
    kvs[192:384] = tkv[1, rest]
    kvs[384:392] = label
    kvw[own, 0:192] = tkv[0, mine]
    kvw[own, 192:384] = tkv[1, mine]
    kvw[own, 384:392] = label
    qs[...] = tq[rest]
    qw[own] = tq[mine]

    pl.semaphore_wait(barrier, len(peers))

    send(kvs, kvw.at[own], kv_sem.at[own], partner)

    def send_block(window, sem, slot, r):
        send(window.at[slot], window.at[1 + r], sem.at[1 + r], pair(1))
        send(window.at[slot], window.at[5 + r], sem.at[5 + r], pair(-1))
        send(window.at[slot], window.at[7 * (1 - r)], sem.at[7 * (1 - r)], pair(4 * r - 2))

    send_block(kvw, kv_sem, own, yl)
    send(qs, qw.at[own], q_sem.at[own], partner)
    arrived(kvw.at[theirs], kv_sem.at[theirs])
    send_block(kvw, kv_sem, theirs, other)

    cotw[yl, head] = cot_ref[...]
    for k in (1, 2, 3):
        send(cot_ref, cotw.at[yl, head], cot_sem.at[yl * 4 + head], along_y(k))
    send(cot_ref, cotw.at[yl, head], cot_sem.at[yl * 4 + head], sibling)
    for k in (1, 3, 2):
        y_from = (y + k) % 4
        row, col = y_from % 2, (y_from // 2) * 2 + core
        arrived(cotw.at[row, col], cot_sem.at[row * 4 + col])
        send(cotw.at[row, col], cotw.at[row, col], cot_sem.at[row * 4 + col], sibling)
    w_copy.wait()
    hi, mid = split2(wv[...])
    wh[...] = hi
    wm[...] = mid
    for k in range(4):
        y_from = (y + k) % 4
        row, col = y_from % 2, (y_from // 2) * 2 + (1 - core)
        arrived(cotw.at[row, col], cot_sem.at[row * 4 + col])
    for row in range(2):
        for col in range(4):
            tile = cotw[row, col]
            hi, mid = split2(tile)
            coth[row * B:(row + 1) * B, col * 384:(col + 1) * 384] = hi
            cotm[row * B:(row + 1) * B, col * 384:(col + 1) * 384] = mid
            hi, mid = split2(tile.T)
            cotth[col * 384:(col + 1) * 384, row * B:(row + 1) * B] = hi
            cottm[col * 384:(col + 1) * 384, row * B:(row + 1) * B] = mid

    do_t[...] = dot_nt(wh[...], coth[...]) + (
        dot_nt(wh[...], cotm[...]) + dot_nt(wm[...], coth[...])
    )
    dow[3] = do_t[:, :B]
    dow[4] = do_t[:, B:]
    arrived(qw.at[theirs], q_sem.at[theirs])

    for s in range(8):
        if s in (3, 4):
            continue
        arrived(kvw.at[s], kv_sem.at[s])

    send_block(qw, q_sem, own, yl)
    send_block(qw, q_sem, theirs, other)

    def send_two(window, sem, base):
        send(window.at[pl.ds(3, 2)], window.at[pl.ds(1, 2)], sem.at[base], pair(1))
        send(window.at[pl.ds(3, 2)], window.at[pl.ds(5, 2)], sem.at[base + 1], pair(-1))
        send(window.at[4], window.at[0], sem.at[base + 2], pair(2))
        send(window.at[3], window.at[7], sem.at[base + 3], pair(-2))

    def arrived_two(window, sem, base):
        arrived(window.at[pl.ds(1, 2)], sem.at[base])
        arrived(window.at[pl.ds(5, 2)], sem.at[base + 1])
        arrived(window.at[0], sem.at[base + 2])
        arrived(window.at[7], sem.at[base + 3])

    send_two(dow, do_sem, 0)

    for r in range(2):
        lab_col[r * B:(r + 1) * B] = jnp.broadcast_to(kvw[3 + r, 384:385], (B, B)).T
        for h in range(2):
            wide = jnp.full((1, B), band_ref[head * 4 + yl * 2 + h], jnp.int32)
            for s in range(8):
                block = jnp.full((1, B), pair_index * 2 - 3 + s, jnp.int32)
                inside = (wide >= abs(s - 3 - r)) & (block >= 0) & (block < 2 * NZ * NX)
                row = jnp.where(inside, kvw[s, 384:385], -1.0)
                lab_row[r * 2 + h, :, s * B:(s + 1) * B] = jnp.broadcast_to(row, (8, B))

    def window(ref, first):
        return pad_rows(
            jnp.concatenate([ref[s, first:first + HD] for s in range(8)], axis=1)
        )

    def middle(ref, first):
        return pad_rows(
            jnp.concatenate([ref[3, first:first + HD], ref[4, first:first + HD]], axis=1)
        ).T

    lane = lax.broadcasted_iota(jnp.int32, (CHUNK, B), 1)

    def allowed(i, r_block, h):
        column = lab_col[pl.ds(pl.multiple_of(i * CHUNK, CHUNK), CHUNK)]
        row = lab_row[r_block * 2 + h, 0:1]
        return jnp.concatenate([column] * 8, axis=1) == row

    for h in range(2):
        s_ref[...] = mul6(middle(qw, h * HD), window(kvw, h * HD))

        def soften(i, carry, h=h):
            rows = pl.ds(pl.multiple_of(i * CHUNK, CHUNK), CHUNK)
            ok = allowed(i, i // (B // CHUNK), h)
            scores = jnp.where(ok, s_ref[rows], -1e30)
            top = jnp.max(scores, axis=1, keepdims=True)
            e = jnp.exp(scores - top)
            total = jnp.sum(e, axis=1, keepdims=True)
            e_ref[h, rows] = e
            hi, mid = split2(e)
            ph[rows] = hi
            pm[rows] = mid
            log_total = top + jnp.log(total)
            kept = jnp.where(lane == h, log_total, col_ref[rows]) if h else log_total
            col_ref[rows] = jnp.where(lane == 2 + h, 1.0 / total, kept)
            return carry

        lax.fori_loop(0, 2 * B // CHUNK, soften, 0)
        mixed = mul_window(ph[...], pm[...], window(kvw, 192 + h * HD))
        mixed = mixed * col_ref[:, 2 + h:3 + h]
        att_t[h * HD:(h + 1) * HD] = mixed.T[:HD]

    stats = col_ref[...].T
    deltas = [
        jnp.sum(do_t[h * HD:(h + 1) * HD] * att_t[h * HD:(h + 1) * HD], axis=0, keepdims=True)
        for h in range(2)
    ]
    rows = jnp.concatenate(
        [stats[0:2], deltas[0], deltas[1], jnp.zeros((4, 2 * B), F32)], axis=0
    )
    stw[3] = rows[:, :B]
    stw[4] = rows[:, B:]
    send_two(stw, st_sem, 0)

    hi, mid = split2(att_t[...].T)
    ath[...] = hi
    atm[...] = mid
    for col in range(4):
        part = mul3(
            ath[...], atm[...],
            wh[:, col * 384:(col + 1) * 384], wm[:, col * 384:(col + 1) * 384],
        )
        po[col % 2, (col // 2) * 2] = part[:B]
        po[col % 2, (col // 2) * 2 + 1] = part[B:]
    send(po.at[1 - core], por, po_sem, sibling)

    def weigh(i, carry):
        rows = pl.ds(pl.multiple_of(i * 192, 64), 192)
        block = mul3(cotth[rows], cottm[rows], ath[...], atm[...])
        for j in range(NX):
            chunk = block[j * 48:(j + 1) * 48]
            mx[j, i, 0:48] = chunk[:, :B]
            mx[j, i, 48:72] = jnp.concatenate([chunk[:24, B:], chunk[24:, B:]], axis=1)
        return carry

    lax.fori_loop(0, NZ, weigh, 0)
    for k in (1, 2, 3):
        send(mx.at[(x + k) % NX], xr.at[k - 1], x_sem.at[k - 1], along_x(k))

    arrived(por, po_sem)
    for t in range(4):
        ps[t] = po[core, t] + por[t]
    for k in (1, 2, 3):
        send(ps.at[(y + k) % 4], pr.at[k - 1], pr_sem.at[k - 1], along_y(k))

    for h in range(2):
        delta_col = jnp.concatenate([rows[2 + h:3 + h], jnp.zeros((7, 2 * B), F32)], axis=0)
        delta_col = jnp.concatenate([delta_col, jnp.zeros((B - 8, 2 * B), F32)], axis=0).T
        col_ref[...] = jnp.where(
            lax.broadcasted_iota(jnp.int32, (2 * B, B), 1) == 4, delta_col[:, 0:1], col_ref[...]
        )
        gradient = jnp.concatenate([dow[3, h * HD:(h + 1) * HD], dow[4, h * HD:(h + 1) * HD]], axis=1)
        dp_ref[...] = mul4(pad_rows(gradient).T, window(kvw, 192 + h * HD))

        def slope(i, carry, h=h):
            at_rows = pl.ds(pl.multiple_of(i * CHUNK, CHUNK), CHUNK)
            column = col_ref[at_rows]
            probs = e_ref[h, at_rows] * column[:, 2 + h:3 + h]
            hi, mid = split2(probs * (dp_ref[at_rows] - column[:, 4:5]))
            ph[at_rows] = hi
            pm[at_rows] = mid
            return carry

        lax.fori_loop(0, 2 * B // CHUNK, slope, 0)
        result = (mul_window(ph[...], pm[...], window(kvw, h * HD)) * SCALE).T[:HD]
        gown[0, h * HD:(h + 1) * HD] = jnp.where(yl == 0, result[:, :B], result[:, B:])
        gsend[0, h * HD:(h + 1) * HD] = jnp.where(yl == 0, result[:, B:], result[:, :B])
    send(gsend.at[0], grecv.at[0], g_sem.at[0], partner)

    for k in (1, 2, 3):
        arrived(xr.at[k - 1], x_sem.at[k - 1])
    xs[...] = mx[x] + xr[0] + xr[1] + xr[2]
    for k in range(1, NZ):
        send(xs.at[(z + k) % NZ], zr.at[k - 1], z_sem.at[k - 1], along_z(k))

    for s in range(8):
        if s in (3, 4):
            continue
        arrived(qw.at[s], q_sem.at[s])
    arrived_two(dow, do_sem, 0)
    arrived_two(stw, st_sem, 0)
    for h in range(2):
        s_ref[...] = mul6(middle(kvw, h * HD), window(qw, h * HD))
        dp_ref[...] = mul4(middle(kvw, 192 + h * HD), window(dow, h * HD))
        log_row = jnp.concatenate([stw[s, h:h + 1] for s in range(8)], axis=1)
        delta_row = jnp.concatenate([stw[s, 2 + h:3 + h] for s in range(8)], axis=1)

        def weigh_keys(i, carry, h=h, log_row=log_row, delta_row=delta_row):
            at_rows = pl.ds(pl.multiple_of(i * CHUNK, CHUNK), CHUNK)
            ok = allowed(i, i // (B // CHUNK), h)
            probs = jnp.exp(jnp.where(ok, s_ref[at_rows] - log_row, -1e30))
            hi, mid = split2(probs)
            ph[at_rows] = hi
            pm[at_rows] = mid
            dp_ref[at_rows] = probs * (dp_ref[at_rows] - delta_row)
            return carry

        lax.fori_loop(0, 2 * B // CHUNK, weigh_keys, 0)
        value_part = mul_window(ph[...], pm[...], window(dow, h * HD)).T[:HD]
        hi, mid = split2(dp_ref[...])
        key_part = mul_window(hi, mid, window(qw, h * HD)).T[:HD]
        for n, result in ((1, key_part), (2, value_part)):
            gown[n, h * HD:(h + 1) * HD] = jnp.where(yl == 0, result[:, :B], result[:, B:])
            gsend[n, h * HD:(h + 1) * HD] = jnp.where(yl == 0, result[:, B:], result[:, :B])
    send(gsend.at[1], grecv.at[1], g_sem.at[1], partner)
    send(gsend.at[2], grecv.at[2], g_sem.at[2], partner)

    for k in (1, 2, 3):
        arrived(pr.at[k - 1], pr_sem.at[k - 1])
    out_ref[...] = ps[y] + pr[0] + pr[1] + pr[2]

    total = xs[z]
    for k in range(1, NZ):
        arrived(zr.at[k - 1], z_sem.at[k - 1])
        total = total + zr[k - 1]
    gsum[...] = total
    send(gsum, yr, y_sem, partner)

    for n, ref in enumerate((gq_ref, gk_ref, gv_ref)):
        arrived(grecv.at[n], g_sem.at[n])
        lower = jnp.where(yl == 0, gown[n], grecv[n])
        upper = jnp.where(yl == 0, grecv[n], gown[n])
        ref[...] = jnp.concatenate([lower, upper], axis=0).T

    arrived(yr, y_sem)
    lower = jnp.where(yl == 0, gsum[...], yr[...])
    upper = jnp.where(yl == 0, yr[...], gsum[...])
    pieces = []
    for part in (lower, upper):
        pieces.append(jnp.where(yl == 0, part[0:24], part[24:48]).T)
        last = part[48:72].T
        pieces.append(jnp.where(yl == 0, last[:64], last[64:]))
    gw_ref[...] = jnp.concatenate(pieces, axis=0)

    for copy in pending:
        copy.wait_send()


SENDS = 66


def shards(query, key, value, segment, band, out_weight, cotangent):
    vmem = pl.BlockSpec(memory_space=pltpu.VMEM)

    def full(*shape):
        return pltpu.VMEM(shape, F32)

    def half(*shape):
        return pltpu.VMEM(shape, BF16)

    block = jax.ShapeDtypeStruct((B, 384), F32)
    dma = pltpu.SemaphoreType.DMA
    return pl.pallas_call(
        kernel,
        out_shape=(block, block, block, block, jax.ShapeDtypeStruct((384, 24), F32)),
        in_specs=[
            vmem, vmem, vmem, vmem,
            pl.BlockSpec(memory_space=pltpu.SMEM),
            pl.BlockSpec(memory_space=pl.ANY),
            vmem,
        ],
        out_specs=[vmem] * 5,
        scratch_shapes=[
            full(384, B), full(2, 384, B), full(392, B), full(8, 392, B),
            full(192, B), full(8, 192, B), full(8, 192, B), full(8, 8, B),
            full(2, 4, B, 384), full(192, 1536), full(2 * B, B), full(4, 8, W8),
            half(2 * B, 1536), half(2 * B, 1536), half(1536, 2 * B), half(1536, 2 * B),
            half(192, 1536), half(192, 1536),
            full(2 * B, W8), full(2, 2 * B, W8), full(2 * B, W8),
            half(2 * B, W8), half(2 * B, W8), full(2 * B, B),
            full(192, 2 * B), full(192, 2 * B), half(2 * B, 192), half(2 * B, 192),
            full(2, 4, B, 384), full(4, B, 384), full(4, B, 384), full(3, B, 384),
            full(NX, NZ, 72, B), full(3, NZ, 72, B), full(NZ, 72, B), full(NZ - 1, 72, B),
            full(72, B), full(72, B), full(3, 192, B), full(3, 192, B), full(3, 192, B),
            dma((SENDS,)), dma((8,)), dma((8,)), dma((4,)), dma((4,)), dma((8,)), dma,
            dma, dma((3,)), dma((3,)), dma((NZ - 1,)), dma((3,)), dma,
        ],
        compiler_params=pltpu.CompilerParams(
            collective_id=0, has_side_effects=True, vmem_limit_bytes=58 * 2**20
        ),
        name="banded_attention",
    )(query, key, value, segment.reshape(1, B), band, out_weight, cotangent)


def solution(mesh):
    in_specs = (
        P("ctx", "head"),
        P("ctx", "head"),
        P("ctx", "head"),
        P("ctx"),
        P(),
        P("head", None),
        P("ctx", "head"),
    )
    out_specs = (
        P("ctx", "head"),
        P("ctx", "head"),
        P("ctx", "head"),
        P("ctx", "head"),
        P("head", "ctx"),
    )
    return jax.shard_map(shards, mesh=mesh, in_specs=in_specs, out_specs=out_specs, check_vma=False)
```

```python
import math

import jax
import jax.numpy as jnp
from jax import lax
from jax.experimental import pallas as pl
from jax.experimental.pallas import tpu as pltpu
from jax.sharding import PartitionSpec as P

MESH = pl.DeviceIdType.MESH
F32 = jnp.float32
BF16 = jnp.bfloat16
HD = 96
SCALE = 1.0 / math.sqrt(HD)
B = 128
W8 = 8 * B
NZ, NX = 8, 4
CHUNK = 32


def split2(x):
    hi = x.astype(BF16)
    return hi, (x - hi.astype(F32)).astype(BF16)


def split3(x):
    hi = x.astype(BF16)
    rest = x - hi.astype(F32)
    mid = rest.astype(BF16)
    return hi, mid, (rest - mid.astype(F32)).astype(BF16)


def dot(a, b):
    return jnp.dot(a, b, preferred_element_type=F32)


def dot_nt(a, b):
    return lax.dot_general(a, b, (((1,), (1,)), ((), ())), preferred_element_type=F32)


def pad_rows(x):
    return jnp.concatenate([x, jnp.zeros((B - HD, x.shape[1]), x.dtype)], axis=0)


def mul6(left, right):
    lh, lm, ll = split3(left)
    rh, rm, rl = split3(right)
    return dot(
        jnp.concatenate([lh, lh, lm, lm, lh, ll], axis=1),
        jnp.concatenate([rh, rm, rh, rm, rl, rh], axis=0),
    )


def mul_window(hi, mid, right):
    rh, rm = split2(right)
    both = jnp.concatenate([rh, rm], axis=0)
    out = dot_nt(hi, both) + dot_nt(mid, both)
    return out[:, :B] + out[:, B:]


def mul_parts(lh, lm, rh, rm):
    return (dot(lh, rh) + dot(lm, rm)) + (dot(lh, rm) + dot(lm, rh))


def kernel(
    q_ref, k_ref, v_ref, seg_ref, band_ref, w_ref, cot_ref,
    out_ref, gq_ref, gk_ref, gv_ref, gw_ref,
    tq, tkv, ks, vs, kw, vw, qs, qw, dow, stw, cotw, wv, lab_col, lab_row,
    coth, cotm, cotl, cotth, cottm, wh, wm, wl,
    s_ref, e_ref, dp_ref, ph, pm, col_ref, att_t, do_t, ath, atm,
    po, por, ps, pf, pr, mx, xfu, xfd, xr, xs, zr, gsum, yr, gown, gsend, grecv,
    ss, k_sem, v_sem, q_sem, do_sem, st_sem, cot_sem, y_sem, po_sem, pr_sem, x_sem, z_sem, g_sem, w_sem,
):
    ctx = lax.axis_index("ctx")
    head = lax.axis_index("head")
    yl = ctx % 2
    pair_index = ctx // 2
    z, x = pair_index // NX, pair_index % NX
    core = head % 2
    y = (head // 2) * 2 + yl
    other = 1 - yl

    def at(z_, x_, y_, c_):
        return ((z_ * NX + x_) * 2 + y_ % 2, (y_ // 2) * 2 + c_)

    def pair(k):
        p = (pair_index + k + NZ * NX) % (NZ * NX)
        return at(p // NX, p % NX, y, core)

    partner = at(z, x, (head // 2) * 2 + other, core)
    sibling = at(z, x, y, 1 - core)

    def along_y(k):
        return at(z, x, (y + k) % 4, core)

    def along_x(k):
        return at(z, (x + k) % NX, y, core)

    def along_z(k):
        return at((z + k) % NZ, x, y, core)

    peers = [pair(k) for k in (1, -1, 2, -2)]
    peers += [along_y(k) for k in (1, 2, 3)] + [sibling]
    peers += [along_x(k) for k in (1, 2, 3)]
    peers += [along_z(k) for k in range(1, NZ)]
    barrier = pltpu.get_barrier_semaphore()
    for peer in peers:
        pl.semaphore_signal(barrier, inc=1, device_id=peer, device_id_type=MESH)

    w_copy = pltpu.make_async_copy(
        w_ref.at[pl.ds(pl.multiple_of(yl * 192, 8), 192)], wv, w_sem
    )
    w_copy.start()

    pending = []

    def send(src, dst, recv_sem, device):
        copy = pltpu.make_async_remote_copy(
            src_ref=src, dst_ref=dst, send_sem=ss.at[len(pending)], recv_sem=recv_sem,
            device_id=device, device_id_type=MESH,
        )
        copy.start()
        pending.append(copy)

    def arrived(dst, recv_sem):
        pltpu.make_async_remote_copy(
            src_ref=dst, dst_ref=dst, send_sem=ss.at[0], recv_sem=recv_sem,
            device_id=partner, device_id_type=MESH,
        ).wait_recv()

    own = 3 + yl
    theirs = 3 + other

    mine = pl.ds(pl.multiple_of(yl * 192, 8), 192)
    rest = pl.ds(pl.multiple_of(other * 192, 8), 192)
    tkv[0] = k_ref[...].T
    label = jnp.broadcast_to((seg_ref[...] + 1).astype(F32), (8, B))
    ks[0:192] = tkv[0, rest]
    ks[192:200] = label
    kw[own, 0:192] = tkv[0, mine]
    kw[own, 192:200] = label
    tkv[1] = v_ref[...].T
    vs[...] = tkv[1, rest]
    vw[own] = tkv[1, mine]
    tq[...] = (q_ref[...] * SCALE).T
    qs[...] = tq[rest]
    qw[own] = tq[mine]

    pl.semaphore_wait(barrier, len(peers))

    def send_block(window, sem, slot, r):
        send(window.at[slot], window.at[1 + r], sem.at[1 + r], pair(1))
        send(window.at[slot], window.at[5 + r], sem.at[5 + r], pair(-1))

    def relay(window, sem):
        arrived(window.at[2], sem.at[2])
        send(window.at[2], window.at[0], sem.at[0], pair(1))
        arrived(window.at[5], sem.at[5])
        send(window.at[5], window.at[7], sem.at[7], pair(-1))

    def arrived_window(window, sem):
        for slot in (1, 6, 0, 7):
            arrived(window.at[slot], sem.at[slot])

    send(ks, kw.at[own], k_sem.at[own], partner)
    send(vs, vw.at[own], v_sem.at[own], partner)
    send_block(kw, k_sem, own, yl)
    send_block(vw, v_sem, own, yl)
    send(qs, qw.at[own], q_sem.at[own], partner)
    cotw[yl, head] = cot_ref[...]
    arrived(kw.at[theirs], k_sem.at[theirs])
    send_block(kw, k_sem, theirs, other)
    arrived(vw.at[theirs], v_sem.at[theirs])
    send_block(vw, v_sem, theirs, other)

    def cot_slot(k, c):
        y_from = (y + k) % 4
        return y_from % 2, (y_from // 2) * 2 + c

    def cot_get(k, c, *part):
        row, col = cot_slot(k, c)
        sem = cot_sem.at[row * 4 + col, part[0].start // 64 if part else 0]
        arrived(cotw.at[(row, col, *part)], sem)

    def cot_send(k, device, *part):
        row, col = cot_slot(k, core)
        piece = cotw.at[(row, col, *part)]
        send(piece, piece, cot_sem.at[row * 4 + col, part[0].start // 64 if part else 0], device)

    halves = pl.ds(0, 64), pl.ds(64, 64)
    cot_send(0, along_y(1))
    cot_send(0, along_y(3))
    cot_send(0, sibling)
    relay(kw, k_sem)
    w_copy.wait()
    hi, mid, low = split3(wv[...])
    wh[...] = hi
    wm[...] = mid
    wl[...] = low
    cot_get(3, core)
    cot_send(3, along_y(1), halves[0])
    cot_get(1, core)
    cot_send(1, along_y(3), halves[1])
    cot_send(3, sibling)
    cot_send(1, sibling)
    relay(vw, v_sem)
    arrived(qw.at[theirs], q_sem.at[theirs])
    send_block(qw, q_sem, own, yl)
    send_block(qw, q_sem, theirs, other)
    arrived_window(kw, k_sem)

    for r in range(2):
        lab_col[r * B:(r + 1) * B] = jnp.broadcast_to(kw[3 + r, 192:193], (B, B)).T
        for h in range(2):
            wide = jnp.full((1, B), band_ref[head * 4 + yl * 2 + h], jnp.int32)
            for s in range(8):
                block = jnp.full((1, B), pair_index * 2 - 3 + s, jnp.int32)
                inside = (wide >= abs(s - 3 - r)) & (block >= 0) & (block < 2 * NZ * NX)
                row = jnp.where(inside, kw[s, 192:193], -1.0)
                lab_row[r * 2 + h, :, s * B:(s + 1) * B] = jnp.broadcast_to(row, (8, B))

    def window(ref, first):
        return pad_rows(
            jnp.concatenate([ref[s, first:first + HD] for s in range(8)], axis=1)
        )

    def middle(ref, first):
        return pad_rows(
            jnp.concatenate([ref[3, first:first + HD], ref[4, first:first + HD]], axis=1)
        ).T

    lane = lax.broadcasted_iota(jnp.int32, (CHUNK, B), 1)

    def allowed(i, r_block, h):
        column = lab_col[pl.ds(pl.multiple_of(i * CHUNK, CHUNK), CHUNK)]
        row = lab_row[r_block * 2 + h, 0:1]
        return jnp.concatenate([column] * 8, axis=1) == row

    for h in range(2):
        s_ref[...] = mul6(middle(qw, h * HD), window(kw, h * HD))

        def soften(i, carry, h=h):
            rows = pl.ds(pl.multiple_of(i * CHUNK, CHUNK), CHUNK)
            ok = allowed(i, i // (B // CHUNK), h)
            scores = jnp.where(ok, s_ref[rows], -1e30)
            top = jnp.max(scores, axis=1, keepdims=True)
            e = jnp.exp(scores - top)
            total = jnp.sum(e, axis=1, keepdims=True)
            e_ref[h, rows] = e
            hi, mid = split2(e)
            ph[h, rows] = hi
            pm[h, rows] = mid
            log_total = top + jnp.log(total)
            kept = jnp.where(lane == h, log_total, col_ref[rows]) if h else log_total
            col_ref[rows] = jnp.where(lane == 2 + h, 1.0 / total, kept)
            return carry

        lax.fori_loop(0, 2 * B // CHUNK, soften, 0, unroll=True)

    for part in halves:
        cot_get(2, core, part)
        cot_send(2, sibling, part)
    for k in (0, 1, 3):
        cot_get(k, 1 - core)
    for part in halves:
        cot_get(2, 1 - core, part)
    for row in range(2):
        for col in range(4):
            tile = cotw[row, col]
            hi, mid, low = split3(tile)
            coth[row * B:(row + 1) * B, col * 384:(col + 1) * 384] = hi
            cotm[row * B:(row + 1) * B, col * 384:(col + 1) * 384] = mid
            cotl[row * B:(row + 1) * B, col * 384:(col + 1) * 384] = low
            hi, mid = split2(tile.T)
            cotth[col * 384:(col + 1) * 384, row * B:(row + 1) * B] = hi
            cottm[col * 384:(col + 1) * 384, row * B:(row + 1) * B] = mid

    arrived_window(vw, v_sem)

    for h in range(2):
        mixed = mul_window(ph[h], pm[h], window(vw, h * HD))
        mixed = mixed * col_ref[:, 2 + h:3 + h]
        att_t[h * HD:(h + 1) * HD] = mixed.T[:HD]

    hi, mid = split2(att_t[...].T)
    ath[...] = hi
    atm[...] = mid
    def weigh(i, carry):
        rows = pl.ds(pl.multiple_of(i * 192, 64), 192)
        slot = (i - z + 2 * NZ - 2) % NZ
        block = mul_parts(cotth[rows], cottm[rows], ath[...], atm[...])
        for j in range(NX):
            chunk = block[j * 48:(j + 1) * 48]
            mx[j, slot, 0:48] = chunk[:, :B]
            mx[j, slot, 48:72] = jnp.concatenate([chunk[:24, B:], chunk[24:, B:]], axis=1)
        return carry

    lax.fori_loop(0, NZ, weigh, 0)
    far = (x + 2) % NX
    up, down = (x + 1) % NX, (x + 3) % NX
    thirds = pl.ds(0, 40), pl.ds(40, 32)
    quads = pl.ds(0, 4), pl.ds(4, 4)
    for n, quad in enumerate(quads):
        send(mx.at[far, quad, thirds[0]], xfu.at[n], x_sem.at[n], along_x(1))
        send(mx.at[far, quad, thirds[1]], xfd.at[n], x_sem.at[2 + n], along_x(3))

    relay(qw, q_sem)
    do_t[...] = (dot_nt(wh[...], coth[...]) + dot_nt(wm[...], cotm[...])) + (
        (dot_nt(wh[...], cotm[...]) + dot_nt(wm[...], coth[...]))
        + (dot_nt(wh[...], cotl[...]) + dot_nt(wl[...], coth[...]))
    )
    dow[3] = do_t[:, :B]
    dow[4] = do_t[:, B:]

    def send_two(window, sem, base):
        send(window.at[pl.ds(3, 2)], window.at[pl.ds(1, 2)], sem.at[base], pair(1))
        send(window.at[pl.ds(3, 2)], window.at[pl.ds(5, 2)], sem.at[base + 1], pair(-1))

    def relay_two(window, sem, base):
        arrived(window.at[pl.ds(1, 2)], sem.at[base])
        send(window.at[2], window.at[0], sem.at[base + 2], pair(1))
        arrived(window.at[pl.ds(5, 2)], sem.at[base + 1])
        send(window.at[5], window.at[7], sem.at[base + 3], pair(-1))

    def arrived_two(window, sem, base):
        arrived(window.at[0], sem.at[base + 2])
        arrived(window.at[7], sem.at[base + 3])

    send_two(dow, do_sem, 0)
    stats = col_ref[...].T
    deltas = [
        jnp.sum(do_t[h * HD:(h + 1) * HD] * att_t[h * HD:(h + 1) * HD], axis=0, keepdims=True)
        for h in range(2)
    ]
    rows = jnp.concatenate(
        [stats[0:2], deltas[0], deltas[1], jnp.zeros((4, 2 * B), F32)], axis=0
    )
    stw[3] = rows[:, :B]
    stw[4] = rows[:, B:]
    send_two(stw, st_sem, 0)
    send(stw.at[4], stw.at[0], st_sem.at[2], pair(2))
    send(stw.at[3], stw.at[7], st_sem.at[3], pair(-2))
    for n, quad in enumerate(quads):
        arrived(xfu.at[n], x_sem.at[n])
        mx[up, quad, thirds[0]] = mx[up, quad, thirds[0]] + xfu[n]
        send(mx.at[up, quad], xr.at[0, n], x_sem.at[4 + n], along_x(1))
        arrived(xfd.at[n], x_sem.at[2 + n])
        mx[down, quad, thirds[1]] = mx[down, quad, thirds[1]] + xfd[n]
        send(mx.at[down, quad], xr.at[1, n], x_sem.at[6 + n], along_x(3))
    relay_two(dow, do_sem, 0)

    for col in range(4):
        part = mul_parts(
            ath[...], atm[...],
            wh[:, col * 384:(col + 1) * 384], wm[:, col * 384:(col + 1) * 384],
        )
        po[col % 2, (col // 2) * 2] = part[:B]
        po[col % 2, (col // 2) * 2 + 1] = part[B:]
    send(po.at[1 - core], por, po_sem, sibling)

    arrived(por, po_sem)
    for t in range(4):
        ps[t] = po[core, t] + por[t]
    far_y, up_y, down_y = (y + 2) % 4, (y + 1) % 4, (y + 3) % 4
    send(ps.at[far_y, halves[0]], pf.at[0], pr_sem.at[0], along_y(1))
    send(ps.at[far_y, halves[1]], pf.at[1], pr_sem.at[1], along_y(3))

    def give(n, h, result):
        gown[n, h] = jnp.where(yl == 0, result[:, :B], result[:, B:])
        gsend[n, h] = jnp.where(yl == 0, result[:, B:], result[:, :B])
        send(gsend.at[n, h], grecv.at[n, h], g_sem.at[n * 2 + h], partner)

    for h in range(2):
        delta_col = jnp.concatenate([rows[2 + h:3 + h], jnp.zeros((7, 2 * B), F32)], axis=0)
        delta_col = jnp.concatenate([delta_col, jnp.zeros((B - 8, 2 * B), F32)], axis=0).T
        col_ref[...] = jnp.where(
            lax.broadcasted_iota(jnp.int32, (2 * B, B), 1) == 4, delta_col[:, 0:1], col_ref[...]
        )
        gradient = jnp.concatenate([dow[3, h * HD:(h + 1) * HD], dow[4, h * HD:(h + 1) * HD]], axis=1)
        dp_ref[...] = mul6(pad_rows(gradient).T, window(vw, h * HD))

        def slope(i, carry, h=h):
            at_rows = pl.ds(pl.multiple_of(i * CHUNK, CHUNK), CHUNK)
            column = col_ref[at_rows]
            probs = e_ref[h, at_rows] * column[:, 2 + h:3 + h]
            hi, mid = split2(probs * (dp_ref[at_rows] - column[:, 4:5]))
            ph[h, at_rows] = hi
            pm[h, at_rows] = mid
            return carry

        lax.fori_loop(0, 2 * B // CHUNK, slope, 0, unroll=True)
        result = (mul_window(ph[h], pm[h], window(kw, h * HD)) * SCALE).T[:HD]
        give(0, h, result)
        if h == 0:
            arrived(pf.at[0], pr_sem.at[0])
            ps[up_y, 0:64] = ps[up_y, 0:64] + pf[0]
            send(ps.at[up_y], pr.at[0], pr_sem.at[2], along_y(1))
            arrived(pf.at[1], pr_sem.at[1])
            ps[down_y, 64:128] = ps[down_y, 64:128] + pf[1]
            send(ps.at[down_y], pr.at[1], pr_sem.at[3], along_y(3))

    def sum_half(n):
        arrived(xr.at[0, n], x_sem.at[4 + n])
        arrived(xr.at[1, n], x_sem.at[6 + n])
        xs[quads[n]] = mx[x, quads[n]] + xr[0, n] + xr[1, n]
        for k in ((4, 3, 5, 2), (6, 7, 1))[n]:
            send(xs.at[(k + 6) % NZ], zr.at[k - 1], z_sem.at[k - 1], along_z(k))

    sum_half(0)

    arrived_window(qw, q_sem)
    arrived(stw.at[pl.ds(1, 2)], st_sem.at[0])
    arrived(stw.at[pl.ds(5, 2)], st_sem.at[1])
    arrived_two(stw, st_sem, 0)
    arrived_two(dow, do_sem, 0)
    for h in range(2):
        s_ref[...] = mul6(middle(kw, h * HD), window(qw, h * HD))
        dp_ref[...] = mul6(middle(vw, h * HD), window(dow, h * HD))
        log_row = jnp.concatenate([stw[s, h:h + 1] for s in range(8)], axis=1)
        delta_row = jnp.concatenate([stw[s, 2 + h:3 + h] for s in range(8)], axis=1)

        def weigh_keys(i, carry, h=h, log_row=log_row, delta_row=delta_row):
            at_rows = pl.ds(pl.multiple_of(i * CHUNK, CHUNK), CHUNK)
            ok = allowed(i, i // (B // CHUNK), h)
            probs = jnp.exp(jnp.where(ok, s_ref[at_rows] - log_row, -1e30))
            hi, mid = split2(probs)
            ph[h, at_rows] = hi
            pm[h, at_rows] = mid
            dp_ref[at_rows] = probs * (dp_ref[at_rows] - delta_row)
            return carry

        lax.fori_loop(0, 2 * B // CHUNK, weigh_keys, 0, unroll=True)
        give(2, h, mul_window(ph[h], pm[h], window(dow, h * HD)).T[:HD])
        hi, mid = split2(dp_ref[...])
        give(1, h, mul_window(hi, mid, window(qw, h * HD)).T[:HD])
        if h == 0:
            sum_half(1)

    arrived(pr.at[0], pr_sem.at[2])
    arrived(pr.at[1], pr_sem.at[3])
    out_ref[...] = ps[y] + pr[0] + pr[1]

    total = xs[6]
    for k in range(1, NZ):
        arrived(zr.at[k - 1], z_sem.at[k - 1])
        total = total + zr[k - 1]
    gsum[...] = total
    send(gsum, yr, y_sem, partner)

    for n, ref in enumerate((gq_ref, gk_ref, gv_ref)):
        for h in range(2):
            arrived(grecv.at[n, h], g_sem.at[n * 2 + h])
        lower = [jnp.where(yl == 0, gown[n, h], grecv[n, h]) for h in range(2)]
        upper = [jnp.where(yl == 0, grecv[n, h], gown[n, h]) for h in range(2)]
        ref[...] = jnp.concatenate(lower + upper, axis=0).T

    arrived(yr, y_sem)
    lower = jnp.where(yl == 0, gsum[...], yr[...])
    upper = jnp.where(yl == 0, yr[...], gsum[...])
    pieces = []
    for part in (lower, upper):
        pieces.append(jnp.where(yl == 0, part[0:24], part[24:48]))
        last = part[48:72]
        pieces.append(jnp.where(yl == 0, last[:, :64], last[:, 64:]))
    gw_ref[...] = jnp.concatenate(pieces, axis=1)

    assert len(pending) == SENDS
    for copy in pending:
        copy.wait_send()


SENDS = 65


def hand_over(*refs):
    for n in range(5):
        refs[5 + n][...] = refs[n][...]


def shards(query, key, value, segment, band, out_weight, cotangent):
    vmem = pl.BlockSpec(memory_space=pltpu.VMEM)

    def full(*shape):
        return pltpu.VMEM(shape, F32)

    def half(*shape):
        return pltpu.VMEM(shape, BF16)

    block = jax.ShapeDtypeStruct((B, 384), F32)
    dma = pltpu.SemaphoreType.DMA
    results = pl.pallas_call(
        kernel,
        out_shape=(block, block, block, block, jax.ShapeDtypeStruct((24, 384), F32)),
        in_specs=[
            vmem, vmem, vmem, vmem,
            pl.BlockSpec(memory_space=pltpu.SMEM),
            pl.BlockSpec(memory_space=pl.ANY),
            vmem,
        ],
        out_specs=[vmem] * 5,
        scratch_shapes=[
            full(384, B), full(2, 384, B), full(200, B), full(192, B), full(8, 200, B), full(8, 192, B),
            full(192, B), full(8, 192, B), full(8, 192, B), full(8, 8, B),
            full(2, 4, B, 384), full(192, 1536), full(2 * B, B), full(4, 8, W8),
            half(2 * B, 1536), half(2 * B, 1536), half(2 * B, 1536), half(1536, 2 * B), half(1536, 2 * B),
            half(192, 1536), half(192, 1536), half(192, 1536),
            full(2 * B, W8), full(2, 2 * B, W8), full(2 * B, W8),
            half(2, 2 * B, W8), half(2, 2 * B, W8), full(2 * B, B),
            full(192, 2 * B), full(192, 2 * B), half(2 * B, 192), half(2 * B, 192),
            full(2, 4, B, 384), full(4, B, 384), full(4, B, 384), full(2, 64, 384), full(2, B, 384),
            full(NX, NZ, 72, B), full(2, 4, 40, B), full(2, 4, 32, B), full(2, 2, 4, 72, B), full(NZ, 72, B), full(NZ - 1, 72, B),
            full(72, B), full(72, B), full(3, 2, HD, B), full(3, 2, HD, B), full(3, 2, HD, B),
            dma((SENDS,)), dma((8,)), dma((8,)), dma((8,)), dma((4,)), dma((4,)), dma((8, 2)), dma,
            dma, dma((4,)), dma((8,)), dma((NZ - 1,)), dma((6,)), dma,
        ],
        compiler_params=pltpu.CompilerParams(
            collective_id=0, has_side_effects=True, vmem_limit_bytes=58 * 2**20
        ),
        name="banded_attention",
    )(query, key, value, segment.reshape(1, B), band, out_weight, cotangent)
    *blocks, weight = pl.pallas_call(
        hand_over,
        out_shape=[jax.ShapeDtypeStruct(r.shape, F32) for r in results],
        in_specs=[vmem] * 5,
        out_specs=[vmem] * 5,
        compiler_params=pltpu.CompilerParams(vmem_limit_bytes=58 * 2**20),
        name="hand_over",
    )(*results)
    return (*blocks, weight.T)


def solution(mesh):
    in_specs = (
        P("ctx", "head"),
        P("ctx", "head"),
        P("ctx", "head"),
        P("ctx"),
        P(),
        P("head", None),
        P("ctx", "head"),
    )
    out_specs = (
        P("ctx", "head"),
        P("ctx", "head"),
        P("ctx", "head"),
        P("ctx", "head"),
        P("head", "ctx"),
    )
    return jax.shard_map(shards, mesh=mesh, in_specs=in_specs, out_specs=out_specs, check_vma=False)
```

```python
import math

import jax
import jax.numpy as jnp
from jax import lax
from jax.experimental import pallas as pl
from jax.experimental.pallas import tpu as pltpu
from jax.sharding import PartitionSpec as P

MESH = pl.DeviceIdType.MESH
F32 = jnp.float32
BF16 = jnp.bfloat16
HD = 96
SCALE = 1.0 / math.sqrt(HD)
B = 128
W8 = 8 * B
NZ, NX = 8, 4
CHUNK = 32


def split2(x):
    hi = x.astype(BF16)
    return hi, (x - hi.astype(F32)).astype(BF16)


def split3(x):
    hi = x.astype(BF16)
    rest = x - hi.astype(F32)
    mid = rest.astype(BF16)
    return hi, mid, (rest - mid.astype(F32)).astype(BF16)


def dot(a, b):
    return jnp.dot(a, b, preferred_element_type=F32)


def dot_nt(a, b):
    return lax.dot_general(a, b, (((1,), (1,)), ((), ())), preferred_element_type=F32)


def pad_rows(x):
    return jnp.concatenate([x, jnp.zeros((B - HD, x.shape[1]), x.dtype)], axis=0)


def mul6(left, right):
    lh, lm, ll = split3(left)
    rh, rm, rl = split3(right)
    return dot(
        jnp.concatenate([lh, lh, lm, lm, lh, ll], axis=1),
        jnp.concatenate([rh, rm, rh, rm, rl, rh], axis=0),
    )


def mul_window(hi, mid, right):
    rh, rm = split2(right)
    both = jnp.concatenate([rh, rm], axis=0)
    out = dot_nt(hi, both) + dot_nt(mid, both)
    return out[:, :B] + out[:, B:]


def mul_parts(lh, lm, rh, rm):
    return (dot(lh, rh) + dot(lm, rm)) + (dot(lh, rm) + dot(lm, rh))


def kernel(
    q_ref, k_ref, v_ref, seg_ref, band_ref, w_ref, cot_ref,
    out_ref, gq_ref, gk_ref, gv_ref, gw_ref,
    tq, tkv, ks, vs, kw, vw, qs, qw, dow, stw, cotw, wv, lab_col, lab_row,
    coth, cotm, cotl, cotth, cottm, wh, wm, wl,
    s_ref, e_ref, dp_ref, ph, pm, col_ref, att_t, do_t, ath, atm,
    po, por, ps, pf, pr, mx, xfu, xfd, xr, xs, zr, gsum, yr, gown, gsend, grecv,
    ss, k_sem, v_sem, q_sem, do_sem, st_sem, cot_sem, y_sem, po_sem, pr_sem, x_sem, z_sem, g_sem, w_sem,
):
    ctx = lax.axis_index("ctx")
    head = lax.axis_index("head")
    yl = ctx % 2
    pair_index = ctx // 2
    z, x = pair_index // NX, pair_index % NX
    core = head % 2
    y = (head // 2) * 2 + yl
    other = 1 - yl

    def at(z_, x_, y_, c_):
        return ((z_ * NX + x_) * 2 + y_ % 2, (y_ // 2) * 2 + c_)

    def pair(k):
        p = (pair_index + k + NZ * NX) % (NZ * NX)
        return at(p // NX, p % NX, y, core)

    partner = at(z, x, (head // 2) * 2 + other, core)
    sibling = at(z, x, y, 1 - core)

    def along_y(k):
        return at(z, x, (y + k) % 4, core)

    def along_x(k):
        return at(z, (x + k) % NX, y, core)

    def along_z(k):
        return at((z + k) % NZ, x, y, core)

    peers = [pair(k) for k in (1, -1, 2, -2)]
    peers += [along_y(1), along_y(3), sibling, along_x(1), along_x(3)]
    peers += [along_z(k) for k in range(1, NZ)]
    barrier = pltpu.get_barrier_semaphore()
    for peer in peers:
        pl.semaphore_signal(barrier, inc=1, device_id=peer, device_id_type=MESH)

    w_copy = pltpu.make_async_copy(
        w_ref.at[pl.ds(pl.multiple_of(yl * 192, 8), 192)], wv, w_sem
    )
    w_copy.start()

    pending = []

    def send(src, dst, recv_sem, device):
        copy = pltpu.make_async_remote_copy(
            src_ref=src, dst_ref=dst, send_sem=ss.at[len(pending)], recv_sem=recv_sem,
            device_id=device, device_id_type=MESH,
        )
        copy.start()
        pending.append(copy)

    def arrived(dst, recv_sem):
        pltpu.make_async_remote_copy(
            src_ref=dst, dst_ref=dst, send_sem=ss.at[0], recv_sem=recv_sem,
            device_id=partner, device_id_type=MESH,
        ).wait_recv()

    own = 3 + yl
    theirs = 3 + other

    mine = pl.ds(pl.multiple_of(yl * 192, 8), 192)
    rest = pl.ds(pl.multiple_of(other * 192, 8), 192)
    tkv[0] = k_ref[...].T
    label = jnp.broadcast_to((seg_ref[...] + 1).astype(F32), (8, B))
    ks[0:192] = tkv[0, rest]
    ks[192:200] = label
    kw[own, 0:192] = tkv[0, mine]
    kw[own, 192:200] = label
    tkv[1] = v_ref[...].T
    vs[...] = tkv[1, rest]
    vw[own] = tkv[1, mine]
    tq[...] = (q_ref[...] * SCALE).T
    qs[...] = tq[rest]
    qw[own] = tq[mine]

    pl.semaphore_wait(barrier, len(peers))

    def send_block(window, sem, slot, r):
        send(window.at[slot], window.at[1 + r], sem.at[1 + r], pair(1))
        send(window.at[slot], window.at[5 + r], sem.at[5 + r], pair(-1))

    def relay(window, sem):
        arrived(window.at[2], sem.at[2])
        send(window.at[2], window.at[0], sem.at[0], pair(1))
        arrived(window.at[5], sem.at[5])
        send(window.at[5], window.at[7], sem.at[7], pair(-1))

    def arrived_window(window, sem):
        for slot in (1, 6, 0, 7):
            arrived(window.at[slot], sem.at[slot])

    send(ks, kw.at[own], k_sem.at[own], partner)
    send(vs, vw.at[own], v_sem.at[own], partner)
    send_block(kw, k_sem, own, yl)
    send_block(vw, v_sem, own, yl)
    send(qs, qw.at[own], q_sem.at[own], partner)
    cotw[yl, head] = cot_ref[...]
    arrived(kw.at[theirs], k_sem.at[theirs])
    send_block(kw, k_sem, theirs, other)
    arrived(vw.at[theirs], v_sem.at[theirs])
    send_block(vw, v_sem, theirs, other)

    def cot_slot(k, c):
        y_from = (y + k) % 4
        return y_from % 2, (y_from // 2) * 2 + c

    def cot_get(k, c, *part):
        row, col = cot_slot(k, c)
        sem = cot_sem.at[row * 4 + col, part[0].start // 64 if part else 0]
        arrived(cotw.at[(row, col, *part)], sem)

    def cot_send(k, device, *part):
        row, col = cot_slot(k, core)
        piece = cotw.at[(row, col, *part)]
        send(piece, piece, cot_sem.at[row * 4 + col, part[0].start // 64 if part else 0], device)

    halves = pl.ds(0, 64), pl.ds(64, 64)
    cot_send(0, along_y(1))
    cot_send(0, along_y(3))
    cot_send(0, sibling)
    relay(kw, k_sem)
    w_copy.wait()
    hi, mid, low = split3(wv[...])
    wh[...] = hi
    wm[...] = mid
    wl[...] = low
    cot_get(3, core)
    cot_send(3, along_y(1), halves[0])
    cot_get(1, core)
    cot_send(1, along_y(3), halves[1])
    cot_send(3, sibling)
    cot_send(1, sibling)
    relay(vw, v_sem)
    arrived(qw.at[theirs], q_sem.at[theirs])
    send_block(qw, q_sem, own, yl)
    send_block(qw, q_sem, theirs, other)
    arrived_window(kw, k_sem)

    for r in range(2):
        lab_col[r * B:(r + 1) * B] = jnp.broadcast_to(kw[3 + r, 192:193], (B, B)).T
        for h in range(2):
            wide = jnp.full((1, B), band_ref[head * 4 + yl * 2 + h], jnp.int32)
            for s in range(8):
                block = jnp.full((1, B), pair_index * 2 - 3 + s, jnp.int32)
                inside = (wide >= abs(s - 3 - r)) & (block >= 0) & (block < 2 * NZ * NX)
                row = jnp.where(inside, kw[s, 192:193], -1.0)
                lab_row[r * 2 + h, :, s * B:(s + 1) * B] = jnp.broadcast_to(row, (8, B))

    def window(ref, first):
        return pad_rows(
            jnp.concatenate([ref[s, first:first + HD] for s in range(8)], axis=1)
        )

    def middle(ref, first):
        return pad_rows(
            jnp.concatenate([ref[3, first:first + HD], ref[4, first:first + HD]], axis=1)
        ).T

    lane = lax.broadcasted_iota(jnp.int32, (CHUNK, B), 1)

    def allowed(i, r_block, h):
        column = lab_col[pl.ds(pl.multiple_of(i * CHUNK, CHUNK), CHUNK)]
        row = lab_row[r_block * 2 + h, 0:1]
        return jnp.concatenate([column] * 8, axis=1) == row

    for h in range(2):
        s_ref[h] = mul6(middle(qw, h * HD), window(kw, h * HD))

        def soften(i, carry, h=h):
            rows = pl.ds(pl.multiple_of(i * CHUNK, CHUNK), CHUNK)
            ok = allowed(i, i // (B // CHUNK), h)
            scores = jnp.where(ok, s_ref[h, rows], -1e30)
            top = jnp.max(scores, axis=1, keepdims=True)
            e = jnp.exp(scores - top)
            total = jnp.sum(e, axis=1, keepdims=True)
            e_ref[h, rows] = e
            hi, mid = split2(e)
            ph[h, rows] = hi
            pm[h, rows] = mid
            log_total = top + jnp.log(total)
            kept = jnp.where(lane == h, log_total, col_ref[rows]) if h else log_total
            col_ref[rows] = jnp.where(lane == 2 + h, 1.0 / total, kept)
            return carry

        lax.fori_loop(0, 2 * B // CHUNK, soften, 0, unroll=True)

    for part in halves:
        cot_get(2, core, part)
        cot_send(2, sibling, part)
    for k in (0, 1, 3):
        cot_get(k, 1 - core)
    for part in halves:
        cot_get(2, 1 - core, part)
    for row in range(2):
        for col in range(4):
            tile = cotw[row, col]
            hi, mid, low = split3(tile)
            coth[row * B:(row + 1) * B, col * 384:(col + 1) * 384] = hi
            cotm[row * B:(row + 1) * B, col * 384:(col + 1) * 384] = mid
            cotl[row * B:(row + 1) * B, col * 384:(col + 1) * 384] = low
            hi, mid = split2(tile.T)
            cotth[col * 384:(col + 1) * 384, row * B:(row + 1) * B] = hi
            cottm[col * 384:(col + 1) * 384, row * B:(row + 1) * B] = mid

    relay(qw, q_sem)
    do_t[...] = (dot_nt(wh[...], coth[...]) + dot_nt(wm[...], cotm[...])) + (
        (dot_nt(wh[...], cotm[...]) + dot_nt(wm[...], coth[...]))
        + (dot_nt(wh[...], cotl[...]) + dot_nt(wl[...], coth[...]))
    )
    dow[3] = do_t[:, :B]
    dow[4] = do_t[:, B:]

    def send_two(window, sem, base):
        send(window.at[pl.ds(3, 2)], window.at[pl.ds(1, 2)], sem.at[base], pair(1))
        send(window.at[pl.ds(3, 2)], window.at[pl.ds(5, 2)], sem.at[base + 1], pair(-1))

    def relay_two(window, sem, base):
        arrived(window.at[pl.ds(1, 2)], sem.at[base])
        send(window.at[2], window.at[0], sem.at[base + 2], pair(1))
        arrived(window.at[pl.ds(5, 2)], sem.at[base + 1])
        send(window.at[5], window.at[7], sem.at[base + 3], pair(-1))

    def arrived_two(window, sem, base):
        arrived(window.at[0], sem.at[base + 2])
        arrived(window.at[7], sem.at[base + 3])

    send_two(dow, do_sem, 0)
    arrived_window(vw, v_sem)

    for h in range(2):
        mixed = mul_window(ph[h], pm[h], window(vw, h * HD))
        mixed = mixed * col_ref[:, 2 + h:3 + h]
        att_t[h * HD:(h + 1) * HD] = mixed.T[:HD]

    hi, mid = split2(att_t[...].T)
    ath[...] = hi
    atm[...] = mid
    def weigh(i, carry):
        rows = pl.ds(pl.multiple_of(i * 192, 64), 192)
        slot = (i - z + 2 * NZ - 2) % NZ
        block = mul_parts(cotth[rows], cottm[rows], ath[...], atm[...])
        for j in range(NX):
            chunk = block[j * 48:(j + 1) * 48]
            mx[j, slot, 0:48] = chunk[:, :B]
            mx[j, slot, 48:72] = jnp.concatenate([chunk[:24, B:], chunk[24:, B:]], axis=1)
        return carry

    lax.fori_loop(0, NZ, weigh, 0)
    far = (x + 2) % NX
    up, down = (x + 1) % NX, (x + 3) % NX
    thirds = pl.ds(0, 40), pl.ds(40, 32)
    quads = pl.ds(0, 4), pl.ds(4, 4)
    for n, quad in enumerate(quads):
        send(mx.at[far, quad, thirds[0]], xfu.at[n], x_sem.at[n], along_x(1))
        send(mx.at[far, quad, thirds[1]], xfd.at[n], x_sem.at[2 + n], along_x(3))

    for col in range(4):
        part = mul_parts(
            ath[...], atm[...],
            wh[:, col * 384:(col + 1) * 384], wm[:, col * 384:(col + 1) * 384],
        )
        po[col % 2, (col // 2) * 2] = part[:B]
        po[col % 2, (col // 2) * 2 + 1] = part[B:]
    send(po.at[1 - core], por, po_sem, sibling)

    stats = col_ref[...].T
    deltas = [
        jnp.sum(do_t[h * HD:(h + 1) * HD] * att_t[h * HD:(h + 1) * HD], axis=0, keepdims=True)
        for h in range(2)
    ]
    rows = jnp.concatenate(
        [stats[0:2], deltas[0], deltas[1], jnp.zeros((4, 2 * B), F32)], axis=0
    )
    stw[3] = rows[:, :B]
    stw[4] = rows[:, B:]
    send_two(stw, st_sem, 0)
    send(stw.at[4], stw.at[0], st_sem.at[2], pair(2))
    send(stw.at[3], stw.at[7], st_sem.at[3], pair(-2))
    for n, quad in enumerate(quads):
        arrived(xfu.at[n], x_sem.at[n])
        mx[up, quad, thirds[0]] = mx[up, quad, thirds[0]] + xfu[n]
        send(mx.at[up, quad], xr.at[0, n], x_sem.at[4 + n], along_x(1))
        arrived(xfd.at[n], x_sem.at[2 + n])
        mx[down, quad, thirds[1]] = mx[down, quad, thirds[1]] + xfd[n]
        send(mx.at[down, quad], xr.at[1, n], x_sem.at[6 + n], along_x(3))
    arrived(por, po_sem)
    for t in range(4):
        ps[t] = po[core, t] + por[t]
    far_y, up_y, down_y = (y + 2) % 4, (y + 1) % 4, (y + 3) % 4
    send(ps.at[far_y, halves[0]], pf.at[0], pr_sem.at[0], along_y(1))
    send(ps.at[far_y, halves[1]], pf.at[1], pr_sem.at[1], along_y(3))

    def give(n, h, result):
        gown[n, h] = jnp.where(yl == 0, result[:, :B], result[:, B:])
        gsend[n, h] = jnp.where(yl == 0, result[:, B:], result[:, :B])
        send(gsend.at[n, h], grecv.at[n, h], g_sem.at[n * 2 + h], partner)

    def sum_half(n):
        arrived(xr.at[0, n], x_sem.at[4 + n])
        arrived(xr.at[1, n], x_sem.at[6 + n])
        xs[quads[n]] = mx[x, quads[n]] + xr[0, n] + xr[1, n]
        for k in ((4, 3, 5, 2), (6, 7, 1))[n]:
            send(xs.at[(k + 6) % NZ], zr.at[k - 1], z_sem.at[k - 1], along_z(k))

    for h in range(2):
        delta_col = jnp.concatenate([rows[2 + h:3 + h], jnp.zeros((7, 2 * B), F32)], axis=0)
        delta_col = jnp.concatenate([delta_col, jnp.zeros((B - 8, 2 * B), F32)], axis=0).T
        col_ref[...] = jnp.where(
            lax.broadcasted_iota(jnp.int32, (2 * B, B), 1) == 4, delta_col[:, 0:1], col_ref[...]
        )
        gradient = jnp.concatenate([dow[3, h * HD:(h + 1) * HD], dow[4, h * HD:(h + 1) * HD]], axis=1)
        dp_ref[...] = mul6(pad_rows(gradient).T, window(vw, h * HD))

        def slope(i, carry, h=h):
            at_rows = pl.ds(pl.multiple_of(i * CHUNK, CHUNK), CHUNK)
            column = col_ref[at_rows]
            probs = e_ref[h, at_rows] * column[:, 2 + h:3 + h]
            hi, mid = split2(probs * (dp_ref[at_rows] - column[:, 4:5]))
            ph[h, at_rows] = hi
            pm[h, at_rows] = mid
            return carry

        lax.fori_loop(0, 2 * B // CHUNK, slope, 0, unroll=True)
        result = (mul_window(ph[h], pm[h], window(kw, h * HD)) * SCALE).T[:HD]
        give(0, h, result)
        if h == 0:
            relay_two(dow, do_sem, 0)
            arrived(pf.at[0], pr_sem.at[0])
            ps[up_y, 0:64] = ps[up_y, 0:64] + pf[0]
            send(ps.at[up_y], pr.at[0], pr_sem.at[2], along_y(1))
            arrived(pf.at[1], pr_sem.at[1])
            ps[down_y, 64:128] = ps[down_y, 64:128] + pf[1]
            send(ps.at[down_y], pr.at[1], pr_sem.at[3], along_y(3))

    sum_half(0)
    arrived_window(qw, q_sem)
    for h in range(2):
        s_ref[h] = mul6(middle(kw, h * HD), window(qw, h * HD))

    sum_half(1)
    arrived(stw.at[pl.ds(1, 2)], st_sem.at[0])
    arrived(stw.at[pl.ds(5, 2)], st_sem.at[1])
    arrived_two(stw, st_sem, 0)
    arrived_two(dow, do_sem, 0)
    for h in range(2):
        dp_ref[...] = mul6(middle(vw, h * HD), window(dow, h * HD))
        log_row = jnp.concatenate([stw[s, h:h + 1] for s in range(8)], axis=1)
        delta_row = jnp.concatenate([stw[s, 2 + h:3 + h] for s in range(8)], axis=1)

        def weigh_keys(i, carry, h=h, log_row=log_row, delta_row=delta_row):
            at_rows = pl.ds(pl.multiple_of(i * CHUNK, CHUNK), CHUNK)
            ok = allowed(i, i // (B // CHUNK), h)
            probs = jnp.exp(jnp.where(ok, s_ref[h, at_rows] - log_row, -1e30))
            hi, mid = split2(probs)
            ph[h, at_rows] = hi
            pm[h, at_rows] = mid
            dp_ref[at_rows] = probs * (dp_ref[at_rows] - delta_row)
            return carry

        lax.fori_loop(0, 2 * B // CHUNK, weigh_keys, 0, unroll=True)
        give(2, h, mul_window(ph[h], pm[h], window(dow, h * HD)).T[:HD])
        hi, mid = split2(dp_ref[...])
        give(1, h, mul_window(hi, mid, window(qw, h * HD)).T[:HD])

    arrived(pr.at[0], pr_sem.at[2])
    arrived(pr.at[1], pr_sem.at[3])
    out_ref[...] = ps[y] + pr[0] + pr[1]

    total = xs[6]
    for k in range(1, NZ):
        arrived(zr.at[k - 1], z_sem.at[k - 1])
        total = total + zr[k - 1]
    gsum[...] = total
    send(gsum, yr, y_sem, partner)

    for n, ref in enumerate((gq_ref, gk_ref, gv_ref)):
        for h in range(2):
            arrived(grecv.at[n, h], g_sem.at[n * 2 + h])
        lower = [jnp.where(yl == 0, gown[n, h], grecv[n, h]) for h in range(2)]
        upper = [jnp.where(yl == 0, grecv[n, h], gown[n, h]) for h in range(2)]
        ref[...] = jnp.concatenate(lower + upper, axis=0).T

    arrived(yr, y_sem)
    lower = jnp.where(yl == 0, gsum[...], yr[...])
    upper = jnp.where(yl == 0, yr[...], gsum[...])
    pieces = []
    for part in (lower, upper):
        pieces.append(jnp.where(yl == 0, part[0:24], part[24:48]))
        last = part[48:72]
        pieces.append(jnp.where(yl == 0, last[:, :64], last[:, 64:]))
    gw_ref[...] = jnp.concatenate(pieces, axis=1)

    assert len(pending) == SENDS
    for copy in pending:
        copy.wait_send()


SENDS = 65


def hand_over(*refs):
    for n in range(5):
        refs[5 + n][...] = refs[n][...]


def shards(query, key, value, segment, band, out_weight, cotangent):
    vmem = pl.BlockSpec(memory_space=pltpu.VMEM)

    def full(*shape):
        return pltpu.VMEM(shape, F32)

    def half(*shape):
        return pltpu.VMEM(shape, BF16)

    block = jax.ShapeDtypeStruct((B, 384), F32)
    dma = pltpu.SemaphoreType.DMA
    results = pl.pallas_call(
        kernel,
        out_shape=(block, block, block, block, jax.ShapeDtypeStruct((24, 384), F32)),
        in_specs=[
            vmem, vmem, vmem, vmem,
            pl.BlockSpec(memory_space=pltpu.SMEM),
            pl.BlockSpec(memory_space=pl.ANY),
            vmem,
        ],
        out_specs=[vmem] * 5,
        scratch_shapes=[
            full(384, B), full(2, 384, B), full(200, B), full(192, B), full(8, 200, B), full(8, 192, B),
            full(192, B), full(8, 192, B), full(8, 192, B), full(8, 8, B),
            full(2, 4, B, 384), full(192, 1536), full(2 * B, B), full(4, 8, W8),
            half(2 * B, 1536), half(2 * B, 1536), half(2 * B, 1536), half(1536, 2 * B), half(1536, 2 * B),
            half(192, 1536), half(192, 1536), half(192, 1536),
            full(2, 2 * B, W8), full(2, 2 * B, W8), full(2 * B, W8),
            half(2, 2 * B, W8), half(2, 2 * B, W8), full(2 * B, B),
            full(192, 2 * B), full(192, 2 * B), half(2 * B, 192), half(2 * B, 192),
            full(2, 4, B, 384), full(4, B, 384), full(4, B, 384), full(2, 64, 384), full(2, B, 384),
            full(NX, NZ, 72, B), full(2, 4, 40, B), full(2, 4, 32, B), full(2, 2, 4, 72, B), full(NZ, 72, B), full(NZ - 1, 72, B),
            full(72, B), full(72, B), full(3, 2, HD, B), full(3, 2, HD, B), full(3, 2, HD, B),
            dma((SENDS,)), dma((8,)), dma((8,)), dma((8,)), dma((4,)), dma((4,)), dma((8, 2)), dma,
            dma, dma((4,)), dma((8,)), dma((NZ - 1,)), dma((6,)), dma,
        ],
        compiler_params=pltpu.CompilerParams(
            collective_id=0, has_side_effects=True, vmem_limit_bytes=58 * 2**20
        ),
        name="banded_attention",
    )(query, key, value, segment.reshape(1, B), band, out_weight, cotangent)
    *blocks, weight = pl.pallas_call(
        hand_over,
        out_shape=[jax.ShapeDtypeStruct(r.shape, F32) for r in results],
        in_specs=[vmem] * 5,
        out_specs=[vmem] * 5,
        compiler_params=pltpu.CompilerParams(vmem_limit_bytes=58 * 2**20),
        name="hand_over",
    )(*results)
    return (*blocks, weight.T)


def solution(mesh):
    in_specs = (
        P("ctx", "head"),
        P("ctx", "head"),
        P("ctx", "head"),
        P("ctx"),
        P(),
        P("head", None),
        P("ctx", "head"),
    )
    out_specs = (
        P("ctx", "head"),
        P("ctx", "head"),
        P("ctx", "head"),
        P("ctx", "head"),
        P("head", "ctx"),
    )
    return jax.shard_map(shards, mesh=mesh, in_specs=in_specs, out_specs=out_specs, check_vma=False)
```

```python
import math

import jax
import jax.numpy as jnp
from jax import lax
from jax.experimental import pallas as pl
from jax.experimental.pallas import tpu as pltpu
from jax.sharding import PartitionSpec as P

MESH = pl.DeviceIdType.MESH
F32 = jnp.float32
BF16 = jnp.bfloat16
HD = 96
SCALE = 1.0 / math.sqrt(HD)
B = 128
W8 = 8 * B
NZ, NX = 8, 4
CHUNK = 32


def split2(x):
    hi = x.astype(BF16)
    return hi, (x - hi.astype(F32)).astype(BF16)


def split3(x):
    hi = x.astype(BF16)
    rest = x - hi.astype(F32)
    mid = rest.astype(BF16)
    return hi, mid, (rest - mid.astype(F32)).astype(BF16)


def dot(a, b):
    return jnp.dot(a, b, preferred_element_type=F32)


def dot_nt(a, b):
    return lax.dot_general(a, b, (((1,), (1,)), ((), ())), preferred_element_type=F32)


def pad_rows(x):
    return jnp.concatenate([x, jnp.zeros((B - HD, x.shape[1]), x.dtype)], axis=0)


def mul6(left, right):
    lh, lm, ll = split3(left)
    rh, rm, rl = split3(right)
    return dot(
        jnp.concatenate([lh, lh, lm, lm, lh, ll], axis=1),
        jnp.concatenate([rh, rm, rh, rm, rl, rh], axis=0),
    )


def mul_window(hi, mid, right):
    rh, rm = split2(right)
    both = jnp.concatenate([rh, rm], axis=0)
    out = dot_nt(hi, both) + dot_nt(mid, both)
    return out[:, :B] + out[:, B:]


def mul_parts(lh, lm, rh, rm):
    return (dot(lh, rh) + dot(lm, rm)) + (dot(lh, rm) + dot(lm, rh))


def kernel(
    q_in, k_in, v_in, seg_ref, band_ref, w_ref, cot_in,
    out_hbm, gq_hbm, gk_hbm, gv_hbm, gw_hbm,
    tq, tkv, ks, vs, kw, vw, qs, qw, dow, stw, cotw, wv, lab_col, lab_row,
    coth, cotm, cotl, cotth, cottm, wh, wm, wl,
    s_ref, e_ref, dp_ref, ph, pm, col_ref, att_t, do_t, ath, atm,
    po, por, ps, pf, pr, mx, xfu, xfd, xr, xs, zr, gsum, yr, gown, gsend, grecv,
    ss, k_sem, v_sem, q_sem, do_sem, st_sem, cot_sem, y_sem, po_sem, pr_sem, x_sem, z_sem, g_sem, w_sem,
    q_ref, k_ref, v_ref, in_sem, out_ref, gq_ref, gk_ref, gv_ref, gw_ref, out_sem,
):
    ctx = lax.axis_index("ctx")
    head = lax.axis_index("head")
    yl = ctx % 2
    pair_index = ctx // 2
    z, x = pair_index // NX, pair_index % NX
    core = head % 2
    y = (head // 2) * 2 + yl
    other = 1 - yl

    def at(z_, x_, y_, c_):
        return ((z_ * NX + x_) * 2 + y_ % 2, (y_ // 2) * 2 + c_)

    def pair(k):
        p = (pair_index + k + NZ * NX) % (NZ * NX)
        return at(p // NX, p % NX, y, core)

    partner = at(z, x, (head // 2) * 2 + other, core)
    sibling = at(z, x, y, 1 - core)

    def along_y(k):
        return at(z, x, (y + k) % 4, core)

    def along_x(k):
        return at(z, (x + k) % NX, y, core)

    def along_z(k):
        return at((z + k) % NZ, x, y, core)

    peers = [pair(k) for k in (1, -1, 2, -2)]
    peers += [along_y(1), along_y(3), sibling, along_x(1), along_x(3)]
    peers += [along_z(k) for k in range(1, NZ)]
    barrier = pltpu.get_barrier_semaphore()
    for peer in peers:
        pl.semaphore_signal(barrier, inc=1, device_id=peer, device_id_type=MESH)

    inputs = [
        pltpu.make_async_copy(src, dst, in_sem.at[n])
        for n, (src, dst) in enumerate(
            ((k_in, k_ref), (v_in, v_ref), (q_in, q_ref), (cot_in, cotw.at[yl, head]))
        )
    ]
    for copy in inputs:
        copy.start()
    w_copy = pltpu.make_async_copy(
        w_ref.at[pl.ds(pl.multiple_of(yl * 192, 8), 192)], wv, w_sem
    )
    w_copy.start()

    pending = []

    def send(src, dst, recv_sem, device):
        copy = pltpu.make_async_remote_copy(
            src_ref=src, dst_ref=dst, send_sem=ss.at[len(pending)], recv_sem=recv_sem,
            device_id=device, device_id_type=MESH,
        )
        copy.start()
        pending.append(copy)

    def arrived(dst, recv_sem):
        pltpu.make_async_remote_copy(
            src_ref=dst, dst_ref=dst, send_sem=ss.at[0], recv_sem=recv_sem,
            device_id=partner, device_id_type=MESH,
        ).wait_recv()

    own = 3 + yl
    theirs = 3 + other

    mine = pl.ds(pl.multiple_of(yl * 192, 8), 192)
    rest = pl.ds(pl.multiple_of(other * 192, 8), 192)
    inputs[0].wait()
    tkv[0] = k_ref[...].T
    label = jnp.broadcast_to((seg_ref[...] + 1).astype(F32), (8, B))
    ks[0:192] = tkv[0, rest]
    ks[192:200] = label
    kw[own, 0:192] = tkv[0, mine]
    kw[own, 192:200] = label
    inputs[1].wait()
    tkv[1] = v_ref[...].T
    vs[...] = tkv[1, rest]
    vw[own] = tkv[1, mine]
    inputs[2].wait()
    tq[...] = (q_ref[...] * SCALE).T
    qs[...] = tq[rest]
    qw[own] = tq[mine]

    pl.semaphore_wait(barrier, len(peers))

    def send_block(window, sem, slot, r):
        send(window.at[slot], window.at[1 + r], sem.at[1 + r], pair(1))
        send(window.at[slot], window.at[5 + r], sem.at[5 + r], pair(-1))

    def relay(window, sem):
        arrived(window.at[2], sem.at[2])
        send(window.at[2], window.at[0], sem.at[0], pair(1))
        arrived(window.at[5], sem.at[5])
        send(window.at[5], window.at[7], sem.at[7], pair(-1))

    def arrived_window(window, sem):
        for slot in (1, 6, 0, 7):
            arrived(window.at[slot], sem.at[slot])

    send(ks, kw.at[own], k_sem.at[own], partner)
    send(vs, vw.at[own], v_sem.at[own], partner)
    send_block(kw, k_sem, own, yl)
    send_block(vw, v_sem, own, yl)
    send(qs, qw.at[own], q_sem.at[own], partner)
    inputs[3].wait()
    arrived(kw.at[theirs], k_sem.at[theirs])
    send_block(kw, k_sem, theirs, other)
    arrived(vw.at[theirs], v_sem.at[theirs])
    send_block(vw, v_sem, theirs, other)

    def cot_slot(k, c):
        y_from = (y + k) % 4
        return y_from % 2, (y_from // 2) * 2 + c

    def cot_get(k, c, *part):
        row, col = cot_slot(k, c)
        sem = cot_sem.at[row * 4 + col, part[0].start // 64 if part else 0]
        arrived(cotw.at[(row, col, *part)], sem)

    def cot_send(k, device, *part):
        row, col = cot_slot(k, core)
        piece = cotw.at[(row, col, *part)]
        send(piece, piece, cot_sem.at[row * 4 + col, part[0].start // 64 if part else 0], device)

    halves = pl.ds(0, 64), pl.ds(64, 64)
    cot_send(0, along_y(1))
    cot_send(0, along_y(3))
    cot_send(0, sibling)
    relay(kw, k_sem)
    w_copy.wait()
    hi, mid, low = split3(wv[...])
    wh[...] = hi
    wm[...] = mid
    wl[...] = low
    cot_get(3, core)
    cot_send(3, along_y(1), halves[0])
    cot_get(1, core)
    cot_send(1, along_y(3), halves[1])
    cot_send(3, sibling)
    cot_send(1, sibling)
    relay(vw, v_sem)
    arrived(qw.at[theirs], q_sem.at[theirs])
    send_block(qw, q_sem, own, yl)
    send_block(qw, q_sem, theirs, other)
    arrived_window(kw, k_sem)

    for r in range(2):
        lab_col[r * B:(r + 1) * B] = jnp.broadcast_to(kw[3 + r, 192:193], (B, B)).T
        for h in range(2):
            wide = jnp.full((1, B), band_ref[head * 4 + yl * 2 + h], jnp.int32)
            for s in range(8):
                block = jnp.full((1, B), pair_index * 2 - 3 + s, jnp.int32)
                inside = (wide >= abs(s - 3 - r)) & (block >= 0) & (block < 2 * NZ * NX)
                row = jnp.where(inside, kw[s, 192:193], -1.0)
                lab_row[r * 2 + h, :, s * B:(s + 1) * B] = jnp.broadcast_to(row, (8, B))

    def window(ref, first):
        return pad_rows(
            jnp.concatenate([ref[s, first:first + HD] for s in range(8)], axis=1)
        )

    def middle(ref, first):
        return pad_rows(
            jnp.concatenate([ref[3, first:first + HD], ref[4, first:first + HD]], axis=1)
        ).T

    lane = lax.broadcasted_iota(jnp.int32, (CHUNK, B), 1)

    def allowed(i, r_block, h):
        column = lab_col[pl.ds(pl.multiple_of(i * CHUNK, CHUNK), CHUNK)]
        row = lab_row[r_block * 2 + h, 0:1]
        return jnp.concatenate([column] * 8, axis=1) == row

    for h in range(2):
        s_ref[h] = mul6(middle(qw, h * HD), window(kw, h * HD))

        def soften(i, carry, h=h):
            rows = pl.ds(pl.multiple_of(i * CHUNK, CHUNK), CHUNK)
            ok = allowed(i, i // (B // CHUNK), h)
            scores = jnp.where(ok, s_ref[h, rows], -1e30)
            top = jnp.max(scores, axis=1, keepdims=True)
            e = jnp.exp(scores - top)
            total = jnp.sum(e, axis=1, keepdims=True)
            e_ref[h, rows] = e
            hi, mid = split2(e)
            ph[h, rows] = hi
            pm[h, rows] = mid
            log_total = top + jnp.log(total)
            kept = jnp.where(lane == h, log_total, col_ref[rows]) if h else log_total
            col_ref[rows] = jnp.where(lane == 2 + h, 1.0 / total, kept)
            return carry

        lax.fori_loop(0, 2 * B // CHUNK, soften, 0, unroll=True)

    for part in halves:
        cot_get(2, core, part)
        cot_send(2, sibling, part)
    for k in (0, 1, 3):
        cot_get(k, 1 - core)
    for part in halves:
        cot_get(2, 1 - core, part)
    for row in range(2):
        for col in range(4):
            tile = cotw[row, col]
            hi, mid, low = split3(tile)
            coth[row * B:(row + 1) * B, col * 384:(col + 1) * 384] = hi
            cotm[row * B:(row + 1) * B, col * 384:(col + 1) * 384] = mid
            cotl[row * B:(row + 1) * B, col * 384:(col + 1) * 384] = low
            hi, mid = split2(tile.T)
            cotth[col * 384:(col + 1) * 384, row * B:(row + 1) * B] = hi
            cottm[col * 384:(col + 1) * 384, row * B:(row + 1) * B] = mid

    relay(qw, q_sem)
    do_t[...] = (dot_nt(wh[...], coth[...]) + dot_nt(wm[...], cotm[...])) + (
        (dot_nt(wh[...], cotm[...]) + dot_nt(wm[...], coth[...]))
        + (dot_nt(wh[...], cotl[...]) + dot_nt(wl[...], coth[...]))
    )
    dow[3] = do_t[:, :B]
    dow[4] = do_t[:, B:]

    def send_two(window, sem, base):
        send(window.at[pl.ds(3, 2)], window.at[pl.ds(1, 2)], sem.at[base], pair(1))
        send(window.at[pl.ds(3, 2)], window.at[pl.ds(5, 2)], sem.at[base + 1], pair(-1))

    def relay_two(window, sem, base):
        arrived(window.at[pl.ds(1, 2)], sem.at[base])
        send(window.at[2], window.at[0], sem.at[base + 2], pair(1))
        arrived(window.at[pl.ds(5, 2)], sem.at[base + 1])
        send(window.at[5], window.at[7], sem.at[base + 3], pair(-1))

    def arrived_two(window, sem, base):
        arrived(window.at[0], sem.at[base + 2])
        arrived(window.at[7], sem.at[base + 3])

    send_two(dow, do_sem, 0)
    arrived_window(vw, v_sem)

    for h in range(2):
        mixed = mul_window(ph[h], pm[h], window(vw, h * HD))
        mixed = mixed * col_ref[:, 2 + h:3 + h]
        att_t[h * HD:(h + 1) * HD] = mixed.T[:HD]

    hi, mid = split2(att_t[...].T)
    ath[...] = hi
    atm[...] = mid
    def weigh(i, carry):
        rows = pl.ds(pl.multiple_of(i * 192, 64), 192)
        slot = (i - z + 2 * NZ - 2) % NZ
        block = mul_parts(cotth[rows], cottm[rows], ath[...], atm[...])
        for j in range(NX):
            chunk = block[j * 48:(j + 1) * 48]
            mx[j, slot, 0:48] = chunk[:, :B]
            mx[j, slot, 48:72] = jnp.concatenate([chunk[:24, B:], chunk[24:, B:]], axis=1)
        return carry

    lax.fori_loop(0, NZ, weigh, 0)
    far = (x + 2) % NX
    up, down = (x + 1) % NX, (x + 3) % NX
    thirds = pl.ds(0, 40), pl.ds(40, 32)
    quads = pl.ds(0, 4), pl.ds(4, 4)
    for n, quad in enumerate(quads):
        send(mx.at[far, quad, thirds[0]], xfu.at[n], x_sem.at[n], along_x(1))
        send(mx.at[far, quad, thirds[1]], xfd.at[n], x_sem.at[2 + n], along_x(3))

    for col in range(4):
        part = mul_parts(
            ath[...], atm[...],
            wh[:, col * 384:(col + 1) * 384], wm[:, col * 384:(col + 1) * 384],
        )
        po[col % 2, (col // 2) * 2] = part[:B]
        po[col % 2, (col // 2) * 2 + 1] = part[B:]
    send(po.at[1 - core], por, po_sem, sibling)

    stats = col_ref[...].T
    deltas = [
        jnp.sum(do_t[h * HD:(h + 1) * HD] * att_t[h * HD:(h + 1) * HD], axis=0, keepdims=True)
        for h in range(2)
    ]
    rows = jnp.concatenate(
        [stats[0:2], deltas[0], deltas[1], jnp.zeros((4, 2 * B), F32)], axis=0
    )
    stw[3] = rows[:, :B]
    stw[4] = rows[:, B:]
    send_two(stw, st_sem, 0)
    send(stw.at[4], stw.at[0], st_sem.at[2], pair(2))
    send(stw.at[3], stw.at[7], st_sem.at[3], pair(-2))
    for n, quad in enumerate(quads):
        arrived(xfu.at[n], x_sem.at[n])
        mx[up, quad, thirds[0]] = mx[up, quad, thirds[0]] + xfu[n]
        send(mx.at[up, quad], xr.at[0, n], x_sem.at[4 + n], along_x(1))
        arrived(xfd.at[n], x_sem.at[2 + n])
        mx[down, quad, thirds[1]] = mx[down, quad, thirds[1]] + xfd[n]
        send(mx.at[down, quad], xr.at[1, n], x_sem.at[6 + n], along_x(3))
    arrived(por, po_sem)
    for t in range(4):
        ps[t] = po[core, t] + por[t]
    far_y, up_y, down_y = (y + 2) % 4, (y + 1) % 4, (y + 3) % 4
    send(ps.at[far_y, halves[0]], pf.at[0], pr_sem.at[0], along_y(1))
    send(ps.at[far_y, halves[1]], pf.at[1], pr_sem.at[1], along_y(3))

    def give(n, h, result):
        gown[n, h] = jnp.where(yl == 0, result[:, :B], result[:, B:])
        gsend[n, h] = jnp.where(yl == 0, result[:, B:], result[:, :B])
        send(gsend.at[n, h], grecv.at[n, h], g_sem.at[n * 2 + h], partner)

    def sum_half(n):
        arrived(xr.at[0, n], x_sem.at[4 + n])
        arrived(xr.at[1, n], x_sem.at[6 + n])
        xs[quads[n]] = mx[x, quads[n]] + xr[0, n] + xr[1, n]
        for k in ((4, 3, 5, 2), (6, 7, 1))[n]:
            send(xs.at[(k + 6) % NZ], zr.at[k - 1], z_sem.at[k - 1], along_z(k))

    for h in range(2):
        delta_col = jnp.concatenate([rows[2 + h:3 + h], jnp.zeros((7, 2 * B), F32)], axis=0)
        delta_col = jnp.concatenate([delta_col, jnp.zeros((B - 8, 2 * B), F32)], axis=0).T
        col_ref[...] = jnp.where(
            lax.broadcasted_iota(jnp.int32, (2 * B, B), 1) == 4, delta_col[:, 0:1], col_ref[...]
        )
        gradient = jnp.concatenate([dow[3, h * HD:(h + 1) * HD], dow[4, h * HD:(h + 1) * HD]], axis=1)
        dp_ref[...] = mul6(pad_rows(gradient).T, window(vw, h * HD))

        def slope(i, carry, h=h):
            at_rows = pl.ds(pl.multiple_of(i * CHUNK, CHUNK), CHUNK)
            column = col_ref[at_rows]
            probs = e_ref[h, at_rows] * column[:, 2 + h:3 + h]
            hi, mid = split2(probs * (dp_ref[at_rows] - column[:, 4:5]))
            ph[h, at_rows] = hi
            pm[h, at_rows] = mid
            return carry

        lax.fori_loop(0, 2 * B // CHUNK, slope, 0, unroll=True)
        result = (mul_window(ph[h], pm[h], window(kw, h * HD)) * SCALE).T[:HD]
        give(0, h, result)
        if h == 0:
            relay_two(dow, do_sem, 0)
            arrived(pf.at[0], pr_sem.at[0])
            ps[up_y, 0:64] = ps[up_y, 0:64] + pf[0]
            send(ps.at[up_y], pr.at[0], pr_sem.at[2], along_y(1))
            arrived(pf.at[1], pr_sem.at[1])
            ps[down_y, 64:128] = ps[down_y, 64:128] + pf[1]
            send(ps.at[down_y], pr.at[1], pr_sem.at[3], along_y(3))

    sum_half(0)
    arrived_window(qw, q_sem)
    for h in range(2):
        s_ref[h] = mul6(middle(kw, h * HD), window(qw, h * HD))

    sum_half(1)
    arrived(stw.at[pl.ds(1, 2)], st_sem.at[0])
    arrived(stw.at[pl.ds(5, 2)], st_sem.at[1])
    arrived_two(stw, st_sem, 0)
    arrived_two(dow, do_sem, 0)
    for h in range(2):
        dp_ref[...] = mul6(middle(vw, h * HD), window(dow, h * HD))
        log_row = jnp.concatenate([stw[s, h:h + 1] for s in range(8)], axis=1)
        delta_row = jnp.concatenate([stw[s, 2 + h:3 + h] for s in range(8)], axis=1)

        def weigh_keys(i, carry, h=h, log_row=log_row, delta_row=delta_row):
            at_rows = pl.ds(pl.multiple_of(i * CHUNK, CHUNK), CHUNK)
            ok = allowed(i, i // (B // CHUNK), h)
            probs = jnp.exp(jnp.where(ok, s_ref[h, at_rows] - log_row, -1e30))
            hi, mid = split2(probs)
            ph[h, at_rows] = hi
            pm[h, at_rows] = mid
            dp_ref[at_rows] = probs * (dp_ref[at_rows] - delta_row)
            return carry

        lax.fori_loop(0, 2 * B // CHUNK, weigh_keys, 0, unroll=True)
        give(2, h, mul_window(ph[h], pm[h], window(dow, h * HD)).T[:HD])
        hi, mid = split2(dp_ref[...])
        give(1, h, mul_window(hi, mid, window(qw, h * HD)).T[:HD])

    written = []

    def write(n, src, dst):
        written.append(pltpu.make_async_copy(src, dst, out_sem.at[n]))
        written[-1].start()

    arrived(pr.at[0], pr_sem.at[2])
    arrived(pr.at[1], pr_sem.at[3])
    out_ref[...] = ps[y] + pr[0] + pr[1]
    write(0, out_ref, out_hbm)

    total = xs[6]
    for k in range(1, NZ):
        arrived(zr.at[k - 1], z_sem.at[k - 1])
        total = total + zr[k - 1]
    gsum[...] = total
    send(gsum, yr, y_sem, partner)

    homes = gq_hbm, gk_hbm, gv_hbm
    for n, ref in enumerate((gq_ref, gk_ref, gv_ref)):
        for h in range(2):
            arrived(grecv.at[n, h], g_sem.at[n * 2 + h])
        lower = [jnp.where(yl == 0, gown[n, h], grecv[n, h]) for h in range(2)]
        upper = [jnp.where(yl == 0, grecv[n, h], gown[n, h]) for h in range(2)]
        ref[...] = jnp.concatenate(lower + upper, axis=0).T
        write(1 + n, ref, homes[n])

    arrived(yr, y_sem)
    lower = jnp.where(yl == 0, gsum[...], yr[...])
    upper = jnp.where(yl == 0, yr[...], gsum[...])
    pieces = []
    for part in (lower, upper):
        pieces.append(jnp.where(yl == 0, part[0:24], part[24:48]))
        last = part[48:72]
        pieces.append(jnp.where(yl == 0, last[:, :64], last[:, 64:]))
    gw_ref[...] = jnp.concatenate(pieces, axis=1)
    write(4, gw_ref, gw_hbm)

    assert len(pending) == SENDS
    for copy in pending:
        copy.wait_send()
    for copy in written:
        copy.wait()


SENDS = 65


def hand_over(*refs):
    for n in range(5):
        refs[5 + n][...] = refs[n][...]


def shards(query, key, value, segment, band, out_weight, cotangent):
    vmem = pl.BlockSpec(memory_space=pltpu.VMEM)
    anywhere = pl.BlockSpec(memory_space=pl.ANY)

    def full(*shape):
        return pltpu.VMEM(shape, F32)

    def half(*shape):
        return pltpu.VMEM(shape, BF16)

    block = jax.ShapeDtypeStruct((B, 384), F32)
    dma = pltpu.SemaphoreType.DMA
    results = pl.pallas_call(
        kernel,
        out_shape=(block, block, block, block, jax.ShapeDtypeStruct((24, 384), F32)),
        in_specs=[
            anywhere, anywhere, anywhere, vmem,
            pl.BlockSpec(memory_space=pltpu.SMEM),
            anywhere, anywhere,
        ],
        out_specs=[anywhere] * 5,
        scratch_shapes=[
            full(384, B), full(2, 384, B), full(200, B), full(192, B), full(8, 200, B), full(8, 192, B),
            full(192, B), full(8, 192, B), full(8, 192, B), full(8, 8, B),
            full(2, 4, B, 384), full(192, 1536), full(2 * B, B), full(4, 8, W8),
            half(2 * B, 1536), half(2 * B, 1536), half(2 * B, 1536), half(1536, 2 * B), half(1536, 2 * B),
            half(192, 1536), half(192, 1536), half(192, 1536),
            full(2, 2 * B, W8), full(2, 2 * B, W8), full(2 * B, W8),
            half(2, 2 * B, W8), half(2, 2 * B, W8), full(2 * B, B),
            full(192, 2 * B), full(192, 2 * B), half(2 * B, 192), half(2 * B, 192),
            full(2, 4, B, 384), full(4, B, 384), full(4, B, 384), full(2, 64, 384), full(2, B, 384),
            full(NX, NZ, 72, B), full(2, 4, 40, B), full(2, 4, 32, B), full(2, 2, 4, 72, B), full(NZ, 72, B), full(NZ - 1, 72, B),
            full(72, B), full(72, B), full(3, 2, HD, B), full(3, 2, HD, B), full(3, 2, HD, B),
            dma((SENDS,)), dma((8,)), dma((8,)), dma((8,)), dma((4,)), dma((4,)), dma((8, 2)), dma,
            dma, dma((4,)), dma((8,)), dma((NZ - 1,)), dma((6,)), dma,
            full(B, 384), full(B, 384), full(B, 384), dma((4,)),
            full(B, 384), full(B, 384), full(B, 384), full(B, 384), full(24, 384), dma((5,)),
        ],
        compiler_params=pltpu.CompilerParams(
            collective_id=0, has_side_effects=True, vmem_limit_bytes=58 * 2**20
        ),
        name="banded_attention",
    )(query, key, value, segment.reshape(1, B), band, out_weight, cotangent)
    *blocks, weight = pl.pallas_call(
        hand_over,
        out_shape=[jax.ShapeDtypeStruct(r.shape, F32) for r in results],
        in_specs=[vmem] * 5,
        out_specs=[vmem] * 5,
        compiler_params=pltpu.CompilerParams(vmem_limit_bytes=58 * 2**20),
        name="hand_over",
    )(*results)
    return (*blocks, weight.T)


def solution(mesh):
    in_specs = (
        P("ctx", "head"),
        P("ctx", "head"),
        P("ctx", "head"),
        P("ctx"),
        P(),
        P("head", None),
        P("ctx", "head"),
    )
    out_specs = (
        P("ctx", "head"),
        P("ctx", "head"),
        P("ctx", "head"),
        P("ctx", "head"),
        P("head", "ctx"),
    )
    return jax.shard_map(shards, mesh=mesh, in_specs=in_specs, out_specs=out_specs, check_vma=False)
```
